32 devices in a mesh: row: 8 (over y, x, core), col: 4 (over z).
Axes of the slice: x: 2, y: 2, z: 4, core: 2. Of those that a mesh axis runs over, the one named last changes fastest.
Arguments:
- parent_sigma: float32 [4, 8, 128, 8, 4, 128], P(None, 'row', None, None, 'col'), as said below
- slot_tile: int32 [8, 2], replicated, may hold values from 0 to 3, as said below
- slot_count: int32 [8], replicated, may hold values from 1 to 2, as said below
- panel: float32 [8, 2, 128, 1024], P('row'), may hold values from -0.25 to 0.25
- sep_factor: float32 [1024, 1024], P('row'), as said below
Outputs:
- sigma_update: float32 [8, 2, 128, 1024], P('row')
- sigma_sep: float32 [1024, 1024], P('row')
The draws below stay inside these ranges and needn't reach their ends.
Inputs may be any that keep to these rules, and one draw needn't show every extreme that they name: `parent_sigma`: symmetric when viewed as a [4096, 4096] matrix. `slot_tile`: the slots of one grid row name distinct tiles in increasing order. `slot_count`: every grid row has a live slot; some grid row has all 2 slots live. `sep_factor`: lower triangular with diagonal entries from 1.5 to 3.
All inputs are finite; a program needn't handle non-finite values.
Results may differ from the reference program's by a relative error of at most 0.00024.
Values sent between devices are 32-bit elements; how exact they have to be, the bound alone decides.
A program may use at most 64 MiB of HBM per device.

```python
import math
import jax
import jax.numpy as jnp
from jax import lax

TB = 128
NB = 512
UCAP = 2
PPT = 4
PQT = 8
PAR = 4096
NS = 2048
SEP = 1024
N_ROW = 8
N_COL = 4


def draw_parent_sigma(key, part):
    base_key = jax.random.fold_in(key, 5)
    square = jax.random.normal(base_key, (PAR, PAR), jnp.float32)
    balanced = (square + square.T) * (0.5 / math.sqrt(2.0))
    clipped = jnp.clip(balanced, -3.0, 3.0)
    return clipped.reshape(PPT, N_ROW, TB, PQT, N_COL, TB).astype(jnp.float32)


def draw_slot_tile(key, part):
    base_key = jax.random.fold_in(key, 11)
    row_keys = jax.random.split(base_key, N_ROW)

    def one_row(row_key):
        return jnp.sort(jax.random.permutation(row_key, PPT)[:UCAP]).astype(jnp.int32)
    return jax.vmap(one_row)(row_keys)


def draw_slot_count(key, part):
    base_key = jax.random.fold_in(key, 23)
    count_key, full_key = jax.random.split(base_key)
    counts = jax.random.randint(count_key, (N_ROW,), 1, UCAP + 1)
    full_row = jax.random.randint(full_key, (), 0, N_ROW)
    return jnp.where(jnp.arange(N_ROW) == full_row, UCAP, counts).astype(jnp.int32)


def draw_sep_factor(key, part):
    base_key = jax.random.fold_in(key, 37)
    diag_key, chain_key, sign_key, far_key = jax.random.split(base_key, 4)
    row_index = jnp.arange(SEP)[:, None]
    col_index = jnp.arange(SEP)[None, :]
    diagonal = jax.random.uniform(diag_key, (SEP, 1), jnp.float32, 1.5, 3.0)
    ratio = jax.random.uniform(chain_key, (SEP, 1), jnp.float32, 0.6, 0.85)
    signs = jnp.where(jax.random.bernoulli(sign_key, 0.5, (SEP, 1)), 1.0, -1.0).astype(jnp.float32)
    far_part = jax.random.normal(far_key, (SEP, SEP), jnp.float32) / math.sqrt(NB)
    same_block = row_index // NB == col_index // NB
    next_below = row_index == col_index + 1
    inside = jnp.where(next_below, signs * ratio * diagonal, far_part)
    below = jnp.where(same_block, inside, far_part)
    return jnp.where(row_index > col_index, below, jnp.where(row_index == col_index, diagonal, 0.0)).astype(jnp.float32)


def level_of(rng, shape, cuts, smallest, high):
    loudness, own = 1.0, jax.random.fold_in(rng, 6)
    for position, blocks in cuts:
        draws = jnp.exp(jax.random.uniform(jax.random.fold_in(own, position), (blocks,), jnp.float32, smallest / len(cuts), high / len(cuts)))
        loudness = loudness * jnp.repeat(draws, shape[position] // blocks).reshape([-1 if axis == position else 1 for axis in range(len(shape))])
    return loudness


def gaussian(stream_key, dims, deviation, limit, pieces=(), held_as=jnp.bfloat16):
    result = deviation * jax.random.normal(stream_key, dims, jnp.float32)
    if pieces:
        result = result * level_of(stream_key, dims, pieces, -0.22, 0.18)
    return jnp.clip(result, -limit, limit).astype(held_as)


def setup_inputs(seed: int = 0) -> dict:
    key_list = jax.random.split(jax.random.key(seed), 6)
    return {
        "parent_sigma": draw_parent_sigma(jax.random.fold_in(key_list[5], 71), 0),
        "slot_tile": draw_slot_tile(jax.random.fold_in(key_list[5], 71), 0),
        "slot_count": draw_slot_count(jax.random.fold_in(key_list[5], 71), 0),
        "panel": gaussian(key_list[3], (N_ROW, UCAP, TB, SEP), NB ** -0.5, 0.25, ((0, 8),), jnp.float32),
        "sep_factor": draw_sep_factor(jax.random.fold_in(key_list[5], 71), 0),
    }


def exact_dot(left, right):
    return jnp.dot(left.astype(jnp.float32), right.astype(jnp.float32), precision=lax.Precision.HIGHEST, preferred_element_type=jnp.float32)

def lower_inverse(triangle):
    identity = jnp.eye(triangle.shape[0], dtype=jnp.float32)
    return jax.scipy.linalg.solve_triangular(triangle, identity, lower=True)

def reference(parent_sigma, slot_tile, slot_count, panel, sep_factor):
    owners = jnp.arange(N_ROW, dtype=jnp.int32)[:, None]
    parent_tiles = (slot_tile * N_ROW + owners).astype(jnp.int32)
    offsets = jnp.arange(TB, dtype=jnp.int32)
    update_rows = (parent_tiles[:, :, None] * TB + offsets[None, None, :]).reshape(-1).astype(jnp.int32)
    live_slots = jnp.arange(UCAP, dtype=jnp.int32)[None, :] < slot_count[:, None]
    live_rows = jnp.broadcast_to(live_slots[:, :, None], (N_ROW, UCAP, TB)).reshape(-1, 1).astype(jnp.float32)
    whole_sigma = parent_sigma.reshape(PAR, PAR)
    sigma_inner = jnp.take(jnp.take(whole_sigma, update_rows, axis=0), update_rows, axis=1)
    strips = panel.reshape(NS, SEP) * live_rows
    first_inv = lower_inverse(sep_factor[:NB, :NB])
    last_inv = lower_inverse(sep_factor[NB:, NB:])
    coupling = exact_dot(sep_factor[NB:, :NB], first_inv)
    last_u = exact_dot(strips[:, NB:], last_inv)
    first_u = exact_dot(strips[:, :NB], first_inv)
    last_y = exact_dot(sigma_inner, last_u)
    sigma_last = exact_dot(last_inv.T, last_inv) + exact_dot(last_u.T, last_y)
    first_y = exact_dot(sigma_inner, first_u) - exact_dot(last_y, coupling)
    sigma_cross = exact_dot(sigma_last, coupling) - exact_dot(last_y.T, first_u)
    sigma_first = exact_dot(first_inv.T, first_inv) + exact_dot(first_u.T, first_y) + exact_dot(coupling.T, sigma_cross)
    sigma_update = (-jnp.concatenate([first_y, last_y], axis=1) * live_rows).reshape(N_ROW, UCAP, TB, SEP)
    upper_rows = jnp.concatenate([sigma_first, -sigma_cross.T], axis=1)
    lower_rows = jnp.concatenate([-sigma_cross, sigma_last], axis=1)
    return (sigma_update, jnp.concatenate([upper_rows, lower_rows], axis=0))
```

```python
import functools

import jax
import jax.numpy as jnp
from jax import lax
from jax.experimental import pallas as pl
from jax.experimental.pallas import tpu as pltpu
from jax.sharding import PartitionSpec as P

MESH = pl.DeviceIdType.MESH
F32 = jnp.float32
BF16 = jnp.bfloat16
VMEM_BYTES = 56 * 1024 * 1024


def halves(x):
    high = x.astype(BF16)
    return high, (x - high.astype(F32)).astype(BF16)


def dot_pieces(left, right):
    (lh, ll), (rh, rl) = left, right
    one = functools.partial(jnp.dot, preferred_element_type=F32)
    return one(lh, rh) + (one(lh, rl) + one(ll, rh))


def dot3(left, right):
    return dot_pieces(halves(left), halves(right))


def exact(left, right):
    return jnp.dot(left, right, precision=lax.Precision.HIGHEST, preferred_element_type=F32)


def partial_kernel(ratio, place, tiles, counts, sigma, panel, masked, part, picked, sems):
    slot_cap, tile, _ = panel.shape[1:]
    my_row, my_col = place[0], place[1]
    n_col = tiles.shape[0] // ratio
    copies = []
    for k in range(ratio * slot_cap):
        step, slot = divmod(k, slot_cap)
        column = tiles[my_col + n_col * step, slot] * ratio + step
        for s in range(slot_cap):
            copy = pltpu.make_async_copy(
                sigma.at[tiles[my_row, s], 0, :, column, 0, :],
                picked.at[k, pl.ds(s * tile, tile)],
                sems.at[k, s],
            )
            copy.start()
            copies.append(copy)
    for s in range(slot_cap):
        live = jnp.where(s < counts[my_row], 1.0, 0.0).astype(F32)
        masked[pl.ds(s * tile, tile), :] = panel[0, s] * live
    strips = halves(masked[...])
    for copy in copies:
        copy.wait()
    for k in range(ratio * slot_cap):
        step, slot = divmod(k, slot_cap)
        live = jnp.where(slot < counts[my_col + n_col * step], 1.0, 0.0).astype(F32)
        block = picked[k].T * live
        part[pl.ds(k * tile, tile), :] = dot_pieces(halves(block), strips)


def base_inverse(block):
    size = block.shape[0]
    row = lax.broadcasted_iota(jnp.int32, block.shape, 0)
    col = lax.broadcasted_iota(jnp.int32, block.shape, 1)
    diagonal = row == col
    inverse = jnp.where(diagonal, 1.0 / jnp.where(diagonal, block, 1.0), 0.0)
    for level in range(size.bit_length() - 1):
        row_block, col_block = row >> level, col >> level
        below = jnp.where((row_block == col_block + 1) & ((row_block & 1) == 1), block, 0.0)
        inverse = inverse - exact(inverse, exact(below, inverse))
    return inverse


def main_kernel(
    n_row, n_col, part, masked, sep, out_update, out_sep,
    pair_in, half_sum, scatter_in, chain, z_full, factor, own_rows, both, stacked, stacked_y,
    s_part, s_pair, s_half, s_in, s_own, s_full,
    pair_sem, scatter_send, scatter_recv, own_send, own_recv, far_send, far_recv, pass_send, pass_recv,
    up_send, down_send, chain_recv, give_send, give_recv,
    s_pair_sem, s_scatter_send, s_scatter_recv, s_give_send, s_give_recv,
):
    me, plane = lax.axis_index("row"), lax.axis_index("col")
    pairs = n_row // 2
    parity, mine = lax.rem(me, 2), lax.div(me, 2)
    sibling = me + 1 - 2 * parity
    width = sep.shape[1]
    sep_rows = sep.shape[0]
    front = masked.shape[0]
    chunk = part.shape[0] // n_row
    per_front = front // chunk
    half_rows = pairs * chunk
    half_width = width // 2

    def remote(src, dst, send, recv, row, col):
        return pltpu.make_async_remote_copy(
            src_ref=src, dst_ref=dst, send_sem=send, recv_sem=recv,
            device_id=(row, col), device_id_type=MESH,
        )

    barrier = pltpu.get_barrier_semaphore()
    for d in range(1, n_row):
        pl.semaphore_signal(barrier, inc=1, device_id=(lax.rem(me + d, n_row), plane), device_id_type=MESH)
    for d in range(1, n_col):
        pl.semaphore_signal(barrier, inc=1, device_id=(me, lax.rem(plane + d, n_col)), device_id_type=MESH)
    pl.semaphore_wait(barrier, n_row + n_col - 2)

    theirs = pl.ds(pl.multiple_of((1 - parity) * half_rows, 8), half_rows)
    ours = pl.ds(pl.multiple_of(parity * half_rows, 8), half_rows)
    pair = remote(part.at[theirs], pair_in, pair_sem.at[0], pair_sem.at[1], sibling, plane)
    pair.start()
    factor[pl.ds(0, half_width), pl.ds(half_width, half_width)] = jnp.zeros((half_width, half_width), F32)
    pair.wait()
    half_sum[...] = part[ours, :] + pair_in[...]
    scatters = []
    for d in range(1, pairs):
        k = lax.rem(mine + d, pairs)
        rows = pl.ds(pl.multiple_of(k * chunk, 8), chunk)
        copy = remote(
            half_sum.at[rows], scatter_in.at[d - 1], scatter_send.at[d - 1], scatter_recv.at[d - 1],
            2 * k + parity, plane,
        )
        copy.start()
        scatters.append(copy)

    own_rows[...] = sep[...]
    whole_tile = sep_rows % 128 == 0
    if whole_tile:
        diagonal = pl.ds(pl.multiple_of(me * sep_rows, 128), sep_rows)
        own_rows[:, diagonal] = base_inverse(sep[:, diagonal])
    columns = (pl.ds(0, half_width), pl.ds(half_width, half_width))

    def rows_of(q):
        return pl.ds(pl.multiple_of(q * sep_rows, 8), sep_rows)

    def each_half(q, action):
        action(0)

        @pl.when(q >= pairs)
        def _():
            action(1)

    def own_copy(h):
        return remote(
            own_rows.at[:, columns[h]], factor.at[rows_of(me), columns[h]],
            own_send.at[h], own_recv.at[h], sibling, plane,
        )

    def far_copy(d, h):
        return remote(
            own_rows.at[:, columns[h]], factor.at[rows_of(me), columns[h]],
            far_send.at[d - 1, h], far_recv.at[d - 1, h],
            2 * lax.rem(mine + d, pairs) + parity, plane,
        )

    def pass_copy(d, h):
        q = 2 * lax.rem(mine + pairs - d, pairs) + parity
        return remote(
            factor.at[rows_of(q), columns[h]], factor.at[rows_of(q), columns[h]],
            pass_send.at[d - 1, h], pass_recv.at[d - 1, h], sibling, plane,
        )

    def far_source(d):
        return 2 * lax.rem(mine + pairs - d, pairs) + parity

    def sibling_source(d):
        return 2 * lax.rem(mine + pairs - d, pairs) + 1 - parity

    def start_rows(h):
        for d in range(1, pairs):
            far_copy(d, h).start()
        own_copy(h).start()

    each_half(me, start_rows)
    factor[rows_of(me), columns[0]] = own_rows[:, columns[0]]

    @pl.when(me >= pairs)
    def _():
        factor[rows_of(me), columns[1]] = own_rows[:, columns[1]]

    total = half_sum[pl.ds(pl.multiple_of(mine * chunk, 8), chunk), :]
    for d in range(1, pairs):
        scatters[d - 1].wait()
        total = total + scatter_in[d - 1]
    chain[plane] = total
    position = parity * pairs + mine
    owner_step = lax.div(position, per_front)
    place = lax.rem(position, per_front)
    z_rows = pl.ds(pl.multiple_of(place * chunk, 8), chunk)

    def up_copy(d):
        c = plane - d
        return remote(chain.at[c], chain.at[c], up_send.at[d], chain_recv.at[c], me, plane + 1)

    def down_copy(d):
        c = plane + d
        return remote(chain.at[c], chain.at[c], down_send.at[d], chain_recv.at[c], me, plane - 1)

    def give_copy(c):
        return remote(
            chain.at[c], z_full.at[z_rows], give_send.at[c], give_recv.at[place], c + n_col * owner_step, plane
        )

    def give(c):
        owner = c + n_col * owner_step

        @pl.when(owner == me)
        def _():
            z_full[z_rows, :] = chain[c]

        @pl.when(owner != me)
        def _():
            give_copy(c).start()

    def forward_rows(d):
        def action(h):
            far_copy(d, h).wait_recv()
            pass_copy(d, h).start()

        each_half(far_source(d), action)

    for d in range(n_col):
        @pl.when(plane >= d)
        def _():
            if d:
                remote(
                    chain.at[plane - d], chain.at[plane - d], up_send.at[d], chain_recv.at[plane - d], me, plane - 1
                ).wait_recv()

            @pl.when(plane + 1 < n_col)
            def _():
                up_copy(d).start()

        @pl.when(plane + d < n_col)
        def _():
            if d:
                remote(
                    chain.at[plane + d], chain.at[plane + d], down_send.at[d], chain_recv.at[plane + d], me, plane + 1
                ).wait_recv()

            @pl.when(plane > 0)
            def _():
                down_copy(d).start()

        @pl.when(plane >= d)
        def _():
            give(plane - d)

        if d:
            @pl.when(plane + d < n_col)
            def _():
                give(plane + d)

        if 0 < d < pairs:
            forward_rows(d)
    for d in range(n_col, pairs):
        forward_rows(d)

    each_half(sibling, lambda h: own_copy(h).wait_recv())
    for d in range(1, pairs):
        each_half(sibling_source(d), lambda h: pass_copy(d, h).wait_recv())
        each_half(far_source(d), lambda h: pass_copy(d, h).wait_send())
    if not whole_tile:
        for j in range(width // 128):
            tile = pl.ds(j * 128, 128)
            factor[tile, tile] = base_inverse(factor[tile, tile])
    size = max(sep_rows, 128) if whole_tile else 128
    while size < width:
        for start in range(0, width, 2 * size):
            first, last = pl.ds(start, size), pl.ds(start + size, size)
            inner = dot3(factor[last, first], factor[first, first])
            factor[last, first] = -dot3(factor[last, last], inner)
        size *= 2

    my_step = lax.div(me, n_col)
    for j in range(per_front):
        source = my_step * per_front + j
        source_row = 2 * lax.rem(source, pairs) + lax.div(source, pairs)

        @pl.when(source_row != me)
        def _():
            rows = pl.ds(j * chunk, chunk)
            remote(
                chain.at[plane], z_full.at[rows], give_send.at[0], give_recv.at[j], sibling, plane
            ).wait_recv()

    both[pl.ds(0, front), :] = masked[...]
    both[pl.ds(front, front), :] = z_full[...]
    block = 256
    for j in range(width // block):
        depth = pl.ds(j * block, width - j * block)
        here = pl.ds(j * block, block)
        product = dot3(both[:, depth], factor[depth, here])
        stacked[pl.ds(0, front), here] = product[:front]
        out_update[:, here] = -product[front:]
    stacked[pl.ds(front, sep_rows), :] = factor[rows_of(me), :]

    s_cols = s_own.shape[1]
    repeat = n_col * s_cols // width
    my_cols = pl.ds(pl.multiple_of(lax.div(plane, repeat) * s_cols, 128), s_cols)
    stacked_y[pl.ds(0, front), :] = -out_update[:, my_cols]
    stacked_y[pl.ds(front, sep_rows), :] = stacked[pl.ds(front, sep_rows), my_cols]
    right = halves(stacked_y[...])
    split = 128 // sep_rows
    for j in range(width // 128):
        left = halves(stacked[:, pl.ds(j * 128, 128)].T)
        product = dot_pieces(left, right)
        for i in range(split):
            q = j * split + i
            s_part[q % 2, q // 2] = product[i * sep_rows:(i + 1) * sep_rows]
    s_pairing = remote(s_part.at[1 - parity], s_pair, s_pair_sem.at[0], s_pair_sem.at[1], sibling, plane)
    s_pairing.start()
    s_pairing.wait()
    s_half[...] = s_part[parity] + s_pair[...]
    scatters_s = []
    for d in range(1, pairs):
        k = lax.rem(mine + d, pairs)
        copy = remote(
            s_half.at[k], s_in.at[d - 1], s_scatter_send.at[d - 1], s_scatter_recv.at[d - 1], 2 * k + parity, plane
        )
        copy.start()
        scatters_s.append(copy)
    total = s_half[mine]
    for d in range(1, pairs):
        scatters_s[d - 1].wait()
        total = total + s_in[d - 1]
    s_own[...] = total
    s_full[:, my_cols] = total

    def s_copy(d):
        return remote(
            s_own, s_full.at[:, my_cols], s_give_send.at[d - 1], s_give_recv.at[lax.div(plane, repeat)],
            me, lax.rem(plane + d, n_col),
        )

    @pl.when(lax.rem(plane, repeat) == 0)
    def _():
        for d in range(1, n_col):
            s_copy(d).start()

    for b in range(width // s_cols):
        source = b * repeat

        @pl.when((source != plane) & (lax.div(plane, repeat) != b))
        def _():
            remote(
                s_own, s_full.at[:, pl.ds(b * s_cols, s_cols)], s_give_send.at[0], s_give_recv.at[b], me, source
            ).wait_recv()

    out_sep[...] = s_full[...]

    @pl.when(lax.rem(plane, repeat) == 0)
    def _():
        for d in range(1, n_col):
            s_copy(d).wait_send()

    def sent_rows(h):
        for d in range(1, pairs):
            far_copy(d, h).wait_send()
        own_copy(h).wait_send()

    each_half(me, sent_rows)
    for d in range(n_col):
        @pl.when((plane >= d) & (plane + 1 < n_col))
        def _():
            up_copy(d).wait_send()

        @pl.when((plane + d < n_col) & (plane > 0))
        def _():
            down_copy(d).wait_send()
    for c in range(n_col):
        @pl.when(c + n_col * owner_step != me)
        def _():
            give_copy(c).wait_send()


def on_device(parent_sigma, slot_tile, slot_count, panel, sep_factor):
    n_row = lax.axis_size("row")
    n_col = lax.axis_size("col")
    ratio = n_row // n_col
    slot_cap, tile, width = panel.shape[1:]
    front = slot_cap * tile
    sep_rows = sep_factor.shape[0]
    place = jnp.stack([lax.axis_index("row"), lax.axis_index("col")]).astype(jnp.int32)
    vmem = pl.BlockSpec(memory_space=pltpu.VMEM)
    smem = pl.BlockSpec(memory_space=pltpu.SMEM)
    masked, part = pl.pallas_call(
        functools.partial(partial_kernel, ratio),
        out_shape=(
            jax.ShapeDtypeStruct((front, width), F32),
            jax.ShapeDtypeStruct((ratio * front, width), F32),
        ),
        in_specs=[smem, smem, smem, pl.BlockSpec(memory_space=pl.ANY), vmem],
        out_specs=(vmem, vmem),
        scratch_shapes=[
            pltpu.VMEM((ratio * slot_cap, front, tile), F32),
            pltpu.SemaphoreType.DMA((ratio * slot_cap, slot_cap)),
        ],
        compiler_params=pltpu.CompilerParams(vmem_limit_bytes=VMEM_BYTES),
    )(place, slot_tile, slot_count, parent_sigma, panel)

    pairs = n_row // 2
    chunk = ratio * front // n_row
    s_cols = max(128, width // n_col)
    dma = pltpu.SemaphoreType.DMA
    update, sep = pl.pallas_call(
        functools.partial(main_kernel, n_row, n_col),
        out_shape=(
            jax.ShapeDtypeStruct((front, width), F32),
            jax.ShapeDtypeStruct((sep_rows, width), F32),
        ),
        in_specs=[vmem] * 3,
        out_specs=(vmem, vmem),
        scratch_shapes=[
            pltpu.VMEM((pairs * chunk, width), F32),
            pltpu.VMEM((pairs * chunk, width), F32),
            pltpu.VMEM((pairs - 1, chunk, width), F32),
            pltpu.VMEM((n_col, chunk, width), F32),
            pltpu.VMEM((front, width), F32),
            pltpu.VMEM((width, width), F32),
            pltpu.VMEM((sep_rows, width), F32),
            pltpu.VMEM((2 * front, width), F32),
            pltpu.VMEM((front + sep_rows, width), F32),
            pltpu.VMEM((front + sep_rows, s_cols), F32),
            pltpu.VMEM((2, pairs, sep_rows, s_cols), F32),
            pltpu.VMEM((pairs, sep_rows, s_cols), F32),
            pltpu.VMEM((pairs, sep_rows, s_cols), F32),
            pltpu.VMEM((pairs - 1, sep_rows, s_cols), F32),
            pltpu.VMEM((sep_rows, s_cols), F32),
            pltpu.VMEM((sep_rows, width), F32),
            dma((2,)), dma((pairs - 1,)), dma((pairs - 1,)), dma((2,)), dma((2,)),
            dma((pairs - 1, 2)), dma((pairs - 1, 2)), dma((pairs - 1, 2)), dma((pairs - 1, 2)),
            dma((n_col,)), dma((n_col,)), dma((n_col,)), dma((n_col,)), dma((front // chunk,)),
            dma((2,)), dma((pairs - 1,)), dma((pairs - 1,)), dma((n_col,)), dma((width // s_cols,)),
        ],
        compiler_params=pltpu.CompilerParams(
            collective_id=0, has_side_effects=True, vmem_limit_bytes=VMEM_BYTES
        ),
    )(part, masked, sep_factor)
    return update.reshape(1, slot_cap, tile, width), sep


def solution(mesh):
    placed = (
        P(None, "row", None, None, "col", None),
        P(),
        P(),
        P("row", None, None, None),
        P("row", None),
    )
    return jax.shard_map(
        on_device,
        mesh=mesh,
        in_specs=placed,
        out_specs=(P("row", None, None, None), P("row", None)),
        check_vma=False,
    )
```

```python
import functools

import jax
import jax.numpy as jnp
from jax import lax
from jax.experimental import pallas as pl
from jax.experimental.pallas import tpu as pltpu
from jax.sharding import PartitionSpec as P

MESH = pl.DeviceIdType.MESH
F32 = jnp.float32
BF16 = jnp.bfloat16
VMEM_BYTES = 56 * 1024 * 1024
VIEWS = 2


def halves(x):
    high = x.astype(BF16)
    return high, (x - high.astype(F32)).astype(BF16)


def dot_pieces(left, right):
    (lh, ll), (rh, rl) = left, right
    one = functools.partial(jnp.dot, preferred_element_type=F32)
    return one(lh, rh) + (one(lh, rl) + one(ll, rh))


def dot3(left, right):
    return dot_pieces(halves(left), halves(right))


def exact(left, right):
    return jnp.dot(left, right, precision=lax.Precision.HIGHEST, preferred_element_type=F32)


def partial_kernel(ratio, place, tiles, counts, sigma, panel, masked, part, picked, sems):
    slot_cap, tile, _ = panel.shape[1:]
    my_row, my_col = place[0], place[1]
    n_col = tiles.shape[0] // ratio
    copies = []
    for k in range(ratio * slot_cap):
        step, slot = divmod(k, slot_cap)
        column = tiles[my_col + n_col * step, slot] * ratio + step
        for s in range(slot_cap):
            copy = pltpu.make_async_copy(
                sigma.at[tiles[my_row, s], 0, :, column, 0, :],
                picked.at[k, pl.ds(s * tile, tile)],
                sems.at[k, s],
            )
            copy.start()
            copies.append(copy)
    for s in range(slot_cap):
        live = jnp.where(s < counts[my_row], 1.0, 0.0).astype(F32)
        masked[pl.ds(s * tile, tile), :] = panel[0, s] * live
    strips = halves(masked[...])
    for copy in copies:
        copy.wait()
    for k in range(ratio * slot_cap):
        step, slot = divmod(k, slot_cap)
        live = jnp.where(slot < counts[my_col + n_col * step], 1.0, 0.0).astype(F32)
        block = picked[k].T * live
        product = dot_pieces(halves(block), strips)
        views, _, _, chunk, view_width = part.shape
        for i in range(tile // chunk):
            q = k * (tile // chunk) + i
            for v in range(views):
                part[v, q % 2, q // 2] = product[
                    i * chunk:(i + 1) * chunk, v * view_width:(v + 1) * view_width
                ]


def base_inverse(block):
    size = block.shape[0]
    row = lax.broadcasted_iota(jnp.int32, block.shape, 0)
    col = lax.broadcasted_iota(jnp.int32, block.shape, 1)
    diagonal = row == col
    inverse = jnp.where(diagonal, 1.0 / jnp.where(diagonal, block, 1.0), 0.0)
    for level in range(size.bit_length() - 1):
        row_block, col_block = row >> level, col >> level
        below = jnp.where((row_block == col_block + 1) & ((row_block & 1) == 1), block, 0.0)
        inverse = inverse - exact(inverse, exact(below, inverse))
    return inverse


def main_kernel(
    n_row, n_col, part, masked, sep, out_update, out_sep,
    pair_in, half_sum, scatter_in, chain, z_full, factor, own_rows, both, stacked, stacked_y,
    s_part, s_pair, s_half, s_in, s_full,
    pair_send, pair_recv, scatter_send, scatter_recv,
    own_send, own_recv, far_send, far_recv, pass_send, pass_recv,
    up_send, down_send, chain_recv, give_send, give_recv,
    s_pair_sem, s_send, s_recv, s_up_send, s_down_send, s_chain_recv,
):
    me, plane = lax.axis_index("row"), lax.axis_index("col")
    pairs = n_row // 2
    bits = pairs.bit_length() - 1
    parity, mine = lax.rem(me, 2), lax.div(me, 2)
    sibling = me + 1 - 2 * parity
    width = sep.shape[1]
    sep_rows = sep.shape[0]
    front = masked.shape[0]
    chunk = half_sum.shape[2]
    views = half_sum.shape[0]
    view_width = width // views

    def remote(src, dst, send, recv, row, col):
        return pltpu.make_async_remote_copy(
            src_ref=src, dst_ref=dst, send_sem=send, recv_sem=recv,
            device_id=(row, col), device_id_type=MESH,
        )

    barrier = pltpu.get_barrier_semaphore()
    for d in range(1, n_row):
        pl.semaphore_signal(barrier, inc=1, device_id=(lax.rem(me + d, n_row), plane), device_id_type=MESH)
    for d in range(1, n_col):
        pl.semaphore_signal(barrier, inc=1, device_id=(me, lax.rem(plane + d, n_col)), device_id_type=MESH)
    pl.semaphore_wait(barrier, n_row + n_col - 2)

    flip = [(1 - 2 * lax.rem(lax.div(mine, 1 << b), 2)) * (1 << b) for b in range(bits)]
    order = [(1 - parity) * flip[s] + parity * flip[bits - 1 - s] for s in range(bits)]

    def moved(steps, offset):
        pair = mine
        for s in range(bits):
            if offset >> s & 1:
                pair = pair + steps[s]
        return pair

    def sums(held, landed, send, recv):
        def copy(offset):
            s = (offset & -offset).bit_length() - 1
            return remote(
                held.at[moved(order, offset)], landed.at[offset - 1], send.at[offset - 1], recv.at[offset - 1],
                2 * (mine + order[s]) + parity, plane,
            )

        def gathered(offset, s):
            total = held[moved(order, offset)]
            for t in range(s):
                copy(offset | 1 << t).wait_recv()
                total = total + landed[(offset | 1 << t) - 1]
            return total

        def phase(s):
            for offset in reversed(range(1 << s, pairs, 2 << s)):
                if s:
                    held[moved(order, offset)] = gathered(offset, s)
                copy(offset).start()

        def finish():
            return gathered(0, bits)

        def drain():
            for offset in range(1, pairs):
                copy(offset).wait_send()

        return phase, finish, drain

    def pair_copy(v):
        return remote(part.at[v, 1 - parity], pair_in.at[v], pair_send.at[v], pair_recv.at[v], sibling, plane)

    for v in range(views):
        pair_copy(v).start()
    block = 256
    for g in range(width // block - 1):
        rest = width - (g + 1) * block
        factor[pl.ds(g * block, block), pl.ds((g + 1) * block, rest)] = jnp.zeros((block, rest), F32)
    reductions = [
        sums(half_sum.at[v], scatter_in.at[v], scatter_send.at[v], scatter_recv.at[v]) for v in range(views)
    ]
    for v in range(views):
        pair_copy(v).wait_recv()
        half_sum[v] = part[v, parity] + pair_in[v]
        reductions[v][0](0)

    own_rows[...] = sep[...]
    whole_tile = sep_rows % 128 == 0
    if whole_tile:
        diagonal = pl.ds(pl.multiple_of(me * sep_rows, 128), sep_rows)
        own_rows[:, diagonal] = base_inverse(sep[:, diagonal])
    for s in range(1, bits):
        for v in range(views):
            reductions[v][0](s)

    def rows_of(q):
        return pl.ds(pl.multiple_of(q * sep_rows, 8), sep_rows)

    def by_width(q, action):
        for g in range(width // block):
            @pl.when(lax.div(q * sep_rows, block) == g)
            def _():
                action(pl.ds(0, (g + 1) * block))

    def row_block(offset):
        return 2 * moved(flip, offset) + parity

    def own_copy(cols):
        return remote(
            own_rows.at[:, cols], factor.at[rows_of(me), cols], own_send.at[0], own_recv.at[0], sibling, plane
        )

    def far_copy(offset, b, cols):
        rows = rows_of(row_block(offset))
        source = factor.at[rows, cols] if offset else own_rows.at[:, cols]
        slot = offset + (1 << b) - 1
        return remote(
            source, factor.at[rows, cols], far_send.at[slot], far_recv.at[slot],
            2 * (mine + flip[b]) + parity, plane,
        )

    def arrived(offset, cols):
        b = offset.bit_length() - 1
        rows = rows_of(row_block(offset))
        remote(
            factor.at[rows, cols], factor.at[rows, cols], far_send.at[offset - 1], far_recv.at[offset - 1],
            2 * (mine + flip[b]) + parity, plane,
        ).wait_recv()

    def pass_copy(offset, cols):
        rows = rows_of(row_block(offset))
        return remote(
            factor.at[rows, cols], factor.at[rows, cols],
            pass_send.at[offset - 1], pass_recv.at[offset - 1], sibling, plane,
        )

    def start_rows(cols):
        for b in range(bits):
            far_copy(0, b, cols).start()
        own_copy(cols).start()
        factor[rows_of(me), cols] = own_rows[:, cols]

    by_width(me, start_rows)

    def forward_rows(offset):
        def action(cols):
            arrived(offset, cols)
            for b in range(offset.bit_length(), bits):
                far_copy(offset, b, cols).start()
            pass_copy(offset, cols).start()

        by_width(row_block(offset), action)

    owner_step = lax.div(me, n_col)
    place = lax.rem(me, n_col)
    z_rows = pl.ds(pl.multiple_of(place * chunk, 8), chunk)

    def view_cols(v):
        return pl.ds(v * view_width, view_width)

    def chain_step(slots, valid, up, down, recv, d):
        below, above = plane - d, plane + d
        if d:
            @pl.when((below >= 0) & valid(below))
            def _():
                ref = slots(below)
                remote(ref, ref, up.at[d], recv.at[below], me, plane - 1).wait_recv()

        @pl.when((below >= 0) & (plane + 1 < n_col) & valid(below))
        def _():
            ref = slots(below)
            remote(ref, ref, up.at[d], recv.at[below], me, plane + 1).start()

        if d:
            @pl.when((above < n_col) & valid(above))
            def _():
                ref = slots(above)
                remote(ref, ref, down.at[d], recv.at[above], me, plane + 1).wait_recv()

        @pl.when((above < n_col) & (plane > 0) & valid(above))
        def _():
            ref = slots(above)
            remote(ref, ref, down.at[d], recv.at[above], me, plane - 1).start()

    def chain_drain(slots, valid, up, down, recv):
        for d in range(n_col):
            below, above = plane - d, plane + d

            @pl.when((below >= 0) & (plane + 1 < n_col) & valid(below))
            def _():
                ref = slots(below)
                remote(ref, ref, up.at[d], recv.at[below], me, plane + 1).wait_send()

            @pl.when((above < n_col) & (plane > 0) & valid(above))
            def _():
                ref = slots(above)
                remote(ref, ref, down.at[d], recv.at[above], me, plane - 1).wait_send()

    def always(c):
        return c >= 0

    def give_copy(v, c):
        return remote(
            chain.at[v, c], z_full.at[z_rows, view_cols(v)], give_send.at[v, c], give_recv.at[v, place],
            c + n_col * owner_step, plane,
        )

    def give(v, c):
        @pl.when(c == place)
        def _():
            z_full[z_rows, view_cols(v)] = chain[v, c]

        @pl.when(c != place)
        def _():
            give_copy(v, c).start()

    def z_chain(v):
        return functools.partial(lambda v, c: chain.at[v, c], v), always, up_send.at[v], down_send.at[v], chain_recv.at[v]

    for d in range(n_col):
        for v in range(views):
            if d == 0:
                chain[v, plane] = reductions[v][1]()
            chain_step(*z_chain(v), d)

            @pl.when(plane >= d)
            def _():
                give(v, plane - d)

            if d:
                @pl.when(plane + d < n_col)
                def _():
                    give(v, plane + d)

        if d + 1 < pairs:
            forward_rows(d + 1)
    for offset in range(n_col + 1, pairs):
        forward_rows(offset)

    by_width(sibling, lambda cols: own_copy(cols).wait_recv())
    for offset in range(1, pairs):
        by_width(row_block(offset) + 1 - 2 * parity, lambda cols: pass_copy(offset, cols).wait_recv())

        def sent(cols):
            for b in range(offset.bit_length(), bits):
                far_copy(offset, b, cols).wait_send()
            pass_copy(offset, cols).wait_send()

        by_width(row_block(offset), sent)
    if not whole_tile:
        for j in range(width // 128):
            tile = pl.ds(j * 128, 128)
            factor[tile, tile] = base_inverse(factor[tile, tile])
    size = max(sep_rows, 128) if whole_tile else 128
    while size < width:
        for start in range(0, width, 2 * size):
            first, last = pl.ds(start, size), pl.ds(start + size, size)
            inner = dot3(factor[last, first], factor[first, first])
            factor[last, first] = -dot3(factor[last, last], inner)
        size *= 2

    for j in range(n_col):
        @pl.when(j != place)
        def _():
            for v in range(views):
                remote(
                    chain.at[v, plane], z_full.at[pl.ds(j * chunk, chunk), view_cols(v)],
                    give_send.at[v, 0], give_recv.at[v, j], sibling, plane,
                ).wait_recv()

    both[pl.ds(0, front), :] = masked[...]
    both[pl.ds(front, front), :] = z_full[...]
    for j in range(width // block):
        depth = pl.ds(j * block, width - j * block)
        here = pl.ds(j * block, block)
        product = dot3(both[:, depth], factor[depth, here])
        stacked[pl.ds(0, front), here] = product[:front]
        out_update[:, here] = -product[front:]
    stacked[pl.ds(front, sep_rows), :] = factor[rows_of(me), :]

    s_cols = s_full.shape[2]
    repeat = n_col * s_cols // width
    my_block = lax.div(plane, repeat)
    my_cols = pl.ds(pl.multiple_of(my_block * s_cols, 128), s_cols)
    stacked_y[pl.ds(0, front), :] = -out_update[:, my_cols]
    stacked_y[pl.ds(front, sep_rows), :] = stacked[pl.ds(front, sep_rows), my_cols]
    right = halves(stacked_y[...])
    split = 128 // sep_rows
    for j in range(width // 128):
        left = halves(stacked[:, pl.ds(j * 128, 128)].T)
        product = dot_pieces(left, right)
        for i in range(split):
            q = j * split + i
            s_part[q % 2, q // 2] = product[i * sep_rows:(i + 1) * sep_rows]
    s_pairing = remote(s_part.at[1 - parity], s_pair, s_pair_sem.at[0], s_pair_sem.at[1], sibling, plane)
    s_pairing.start()
    s_pairing.wait()
    s_half[...] = s_part[parity] + s_pair[...]
    s_phase, s_finish, s_drain = sums(s_half, s_in, s_send, s_recv)
    for s in range(bits):
        s_phase(s)

    def first_of_block(c):
        return lax.rem(c, repeat) == 0

    total = s_finish()

    @pl.when(first_of_block(plane))
    def _():
        s_full[my_block] = total

    s_chain = (lambda c: s_full.at[lax.div(c, repeat)]), first_of_block, s_up_send, s_down_send, s_chain_recv
    for d in range(n_col):
        chain_step(*s_chain, d)
    for j in range(width // s_cols):
        out_sep[:, pl.ds(j * s_cols, s_cols)] = s_full[j]

    s_drain()
    chain_drain(*s_chain)
    for v in range(views):
        pair_copy(v).wait_send()
        reductions[v][2]()
        chain_drain(*z_chain(v))
        for c in range(n_col):
            @pl.when(c != place)
            def _():
                give_copy(v, c).wait_send()

    def sent_rows(cols):
        for b in range(bits):
            far_copy(0, b, cols).wait_send()
        own_copy(cols).wait_send()

    by_width(me, sent_rows)


def on_device(parent_sigma, slot_tile, slot_count, panel, sep_factor):
    n_row = lax.axis_size("row")
    n_col = lax.axis_size("col")
    ratio = n_row // n_col
    slot_cap, tile, width = panel.shape[1:]
    front = slot_cap * tile
    sep_rows = sep_factor.shape[0]
    place = jnp.stack([lax.axis_index("row"), lax.axis_index("col")]).astype(jnp.int32)
    vmem = pl.BlockSpec(memory_space=pltpu.VMEM)
    smem = pl.BlockSpec(memory_space=pltpu.SMEM)
    pairs = n_row // 2
    chunk = ratio * front // n_row
    views = VIEWS
    s_cols = max(128, width // n_col)
    masked, part = pl.pallas_call(
        functools.partial(partial_kernel, ratio),
        out_shape=(
            jax.ShapeDtypeStruct((front, width), F32),
            jax.ShapeDtypeStruct((views, 2, pairs, chunk, width // views), F32),
        ),
        in_specs=[smem, smem, smem, pl.BlockSpec(memory_space=pl.ANY), vmem],
        out_specs=(vmem, vmem),
        scratch_shapes=[
            pltpu.VMEM((ratio * slot_cap, front, tile), F32),
            pltpu.SemaphoreType.DMA((ratio * slot_cap, slot_cap)),
        ],
        compiler_params=pltpu.CompilerParams(vmem_limit_bytes=VMEM_BYTES),
    )(place, slot_tile, slot_count, parent_sigma, panel)

    dma = pltpu.SemaphoreType.DMA
    update, sep = pl.pallas_call(
        functools.partial(main_kernel, n_row, n_col),
        out_shape=(
            jax.ShapeDtypeStruct((front, width), F32),
            jax.ShapeDtypeStruct((sep_rows, width), F32),
        ),
        in_specs=[vmem] * 3,
        out_specs=(vmem, vmem),
        scratch_shapes=[
            pltpu.VMEM((views, pairs, chunk, width // views), F32),
            pltpu.VMEM((views, pairs, chunk, width // views), F32),
            pltpu.VMEM((views, pairs - 1, chunk, width // views), F32),
            pltpu.VMEM((views, n_col, chunk, width // views), F32),
            pltpu.VMEM((front, width), F32),
            pltpu.VMEM((width, width), F32),
            pltpu.VMEM((sep_rows, width), F32),
            pltpu.VMEM((2 * front, width), F32),
            pltpu.VMEM((front + sep_rows, width), F32),
            pltpu.VMEM((front + sep_rows, s_cols), F32),
            pltpu.VMEM((2, pairs, sep_rows, s_cols), F32),
            pltpu.VMEM((pairs, sep_rows, s_cols), F32),
            pltpu.VMEM((pairs, sep_rows, s_cols), F32),
            pltpu.VMEM((pairs - 1, sep_rows, s_cols), F32),
            pltpu.VMEM((width // s_cols, sep_rows, s_cols), F32),
            dma((views,)), dma((views,)), dma((views, pairs - 1)), dma((views, pairs - 1)),
            dma((1,)), dma((1,)), dma((2 * pairs,)), dma((pairs - 1,)), dma((pairs - 1,)), dma((pairs - 1,)),
            dma((views, n_col)), dma((views, n_col)), dma((views, n_col)),
            dma((views, n_col)), dma((views, n_col)),
            dma((2,)), dma((pairs - 1,)), dma((pairs - 1,)), dma((n_col,)), dma((n_col,)), dma((n_col,)),
        ],
        compiler_params=pltpu.CompilerParams(
            collective_id=0, has_side_effects=True, vmem_limit_bytes=VMEM_BYTES
        ),
    )(part, masked, sep_factor)
    return update.reshape(1, slot_cap, tile, width), sep


def solution(mesh):
    placed = (
        P(None, "row", None, None, "col", None),
        P(),
        P(),
        P("row", None, None, None),
        P("row", None),
    )
    return jax.shard_map(
        on_device,
        mesh=mesh,
        in_specs=placed,
        out_specs=(P("row", None, None, None), P("row", None)),
        check_vma=False,
    )
```

```python
import functools

import jax
import jax.numpy as jnp
from jax import lax
from jax.experimental import pallas as pl
from jax.experimental.pallas import tpu as pltpu
from jax.sharding import PartitionSpec as P

MESH = pl.DeviceIdType.MESH
F32 = jnp.float32
BF16 = jnp.bfloat16
VMEM_BYTES = 56 * 1024 * 1024
VIEWS = 2


def halves(x):
    high = x.astype(BF16)
    return high, (x - high.astype(F32)).astype(BF16)


def dot_pieces(left, right):
    (lh, ll), (rh, rl) = left, right
    one = functools.partial(jnp.dot, preferred_element_type=F32)
    return one(lh, rh) + (one(lh, rl) + one(ll, rh))


def dot3(left, right):
    return dot_pieces(halves(left), halves(right))


def exact(left, right):
    return jnp.dot(left, right, precision=lax.Precision.HIGHEST, preferred_element_type=F32)


def base_inverse(block):
    size = block.shape[0]
    row = lax.broadcasted_iota(jnp.int32, block.shape, 0)
    col = lax.broadcasted_iota(jnp.int32, block.shape, 1)
    diagonal = row == col
    inverse = jnp.where(diagonal, 1.0 / jnp.where(diagonal, block, 1.0), 0.0)
    for level in range(size.bit_length() - 1):
        row_block, col_block = row >> level, col >> level
        below = jnp.where((row_block == col_block + 1) & ((row_block & 1) == 1), block, 0.0)
        inverse = inverse - exact(inverse, exact(below, inverse))
    return inverse


def main_kernel(
    n_row, n_col, tiles, counts, sigma, panel, sep, out_update, out_sep,
    part, pair_in, half_sum, scatter_in, chain, z_full, factor, own_rows,
    strips_high, strips_low, inverse_high, inverse_low, left_high, left_low, stacked, stacked_y,
    s_part, s_pair, s_half, s_in, s_full,
    pair_send, pair_recv, scatter_send, scatter_recv,
    own_send, own_recv, far_send, far_recv, pass_send, pass_recv,
    up_send, down_send, chain_recv, give_send, give_recv,
    s_pair_send, s_pair_recv, s_send, s_recv, s_up_send, s_down_send, s_chain_recv,
):
    me, plane = lax.axis_index("row"), lax.axis_index("col")
    pairs = n_row // 2
    bits = pairs.bit_length() - 1
    parity, mine = lax.rem(me, 2), lax.div(me, 2)
    sibling = me + 1 - 2 * parity
    width = sep.shape[1]
    sep_rows = sep.shape[0]
    slot_cap, tile = panel.shape[1], panel.shape[2]
    front = slot_cap * tile
    ratio = n_row // n_col
    parent_cols = sigma.shape[2]
    chunk = half_sum.shape[2]
    views = half_sum.shape[0]
    view_width = width // views

    def remote(src, dst, send, recv, row, col):
        return pltpu.make_async_remote_copy(
            src_ref=src, dst_ref=dst, send_sem=send, recv_sem=recv,
            device_id=(row, col), device_id_type=MESH,
        )

    barrier = pltpu.get_barrier_semaphore()
    for d in range(1, n_row):
        pl.semaphore_signal(barrier, inc=1, device_id=(lax.rem(me + d, n_row), plane), device_id_type=MESH)
    for d in range(1, n_col):
        pl.semaphore_signal(barrier, inc=1, device_id=(me, lax.rem(plane + d, n_col)), device_id_type=MESH)
    pl.semaphore_wait(barrier, n_row + n_col - 2)

    flip = [(1 - 2 * lax.rem(lax.div(mine, 1 << b), 2)) * (1 << b) for b in range(bits)]
    order = [(1 - parity) * flip[s] + parity * flip[bits - 1 - s] for s in range(bits)]

    def moved(steps, offset):
        pair = mine
        for s in range(bits):
            if offset >> s & 1:
                pair = pair + steps[s]
        return pair

    def sums(held, landed, send, recv):
        def copy(offset):
            s = (offset & -offset).bit_length() - 1
            return remote(
                held.at[moved(order, offset)], landed.at[offset - 1], send.at[offset - 1], recv.at[offset - 1],
                2 * (mine + order[s]) + parity, plane,
            )

        def gathered(offset, s):
            total = held[moved(order, offset)]
            for t in range(s):
                copy(offset | 1 << t).wait_recv()
                total = total + landed[(offset | 1 << t) - 1]
            return total

        def phase(s):
            for offset in reversed(range(1 << s, pairs, 2 << s)):
                if s:
                    held[moved(order, offset)] = gathered(offset, s)
                copy(offset).start()

        def finish():
            return gathered(0, bits)

        def drain():
            for offset in range(1, pairs):
                copy(offset).wait_send()

        return phase, finish, drain

    def pair_copy(v):
        return remote(part.at[v, 1 - parity], pair_in.at[v], pair_send.at[v], pair_recv.at[v], sibling, plane)

    for s in range(slot_cap):
        live = jnp.where(s < counts[me], 1.0, 0.0).astype(F32)
        rows = pl.ds(s * tile, tile)
        strips_high[rows, :], strips_low[rows, :] = halves(panel[0, s] * live)
    picked = []
    for k in range(ratio * slot_cap):
        step, slot = divmod(k, slot_cap)
        owner = plane + n_col * step
        column = tiles[owner, slot] * ratio + step
        live = jnp.where(slot < counts[owner], 1.0, 0.0).astype(F32)
        stored = [sigma[tiles[me, s], :, column, :] for s in range(slot_cap)]
        picked.append(halves(jnp.concatenate(stored, axis=0).T * live))
    for v in range(views):
        here = pl.ds(v * view_width, view_width)
        right = strips_high[:, here], strips_low[:, here]
        for k in range(ratio * slot_cap):
            product = dot_pieces(picked[k], right)
            for i in range(tile // chunk):
                q = k * (tile // chunk) + i
                part[v, q % 2, q // 2] = product[i * chunk:(i + 1) * chunk]
        pair_copy(v).start()
    block = 256
    for g in range(width // block - 1):
        rest = width - (g + 1) * block
        factor[pl.ds(g * block, block), pl.ds((g + 1) * block, rest)] = jnp.zeros((block, rest), F32)
    reductions = [
        sums(half_sum.at[v], scatter_in.at[v], scatter_send.at[v], scatter_recv.at[v]) for v in range(views)
    ]
    for v in range(views):
        pair_copy(v).wait_recv()
        half_sum[v] = part[v, parity] + pair_in[v]
        reductions[v][0](0)

    own_rows[...] = sep[...]
    whole_tile = sep_rows % 128 == 0
    if whole_tile:
        diagonal = pl.ds(pl.multiple_of(me * sep_rows, 128), sep_rows)
        own_rows[:, diagonal] = base_inverse(sep[:, diagonal])
    for s in range(1, bits):
        for v in range(views):
            reductions[v][0](s)

    def rows_of(q):
        return pl.ds(pl.multiple_of(q * sep_rows, 8), sep_rows)

    def by_width(q, action):
        for g in range(width // block):
            @pl.when(lax.div(q * sep_rows, block) == g)
            def _():
                action(pl.ds(0, (g + 1) * block))

    def row_block(offset):
        return 2 * moved(flip, offset) + parity

    def own_copy(cols):
        return remote(
            own_rows.at[:, cols], factor.at[rows_of(me), cols], own_send.at[0], own_recv.at[0], sibling, plane
        )

    def far_copy(offset, b, cols):
        rows = rows_of(row_block(offset))
        source = factor.at[rows, cols] if offset else own_rows.at[:, cols]
        slot = offset + (1 << b) - 1
        return remote(
            source, factor.at[rows, cols], far_send.at[slot], far_recv.at[slot],
            2 * (mine + flip[b]) + parity, plane,
        )

    def arrived(offset, cols):
        b = offset.bit_length() - 1
        rows = rows_of(row_block(offset))
        remote(
            factor.at[rows, cols], factor.at[rows, cols], far_send.at[offset - 1], far_recv.at[offset - 1],
            2 * (mine + flip[b]) + parity, plane,
        ).wait_recv()

    def pass_copy(offset, cols):
        rows = rows_of(row_block(offset))
        return remote(
            factor.at[rows, cols], factor.at[rows, cols],
            pass_send.at[offset - 1], pass_recv.at[offset - 1], sibling, plane,
        )

    def start_rows(cols):
        for b in range(bits):
            far_copy(0, b, cols).start()
        own_copy(cols).start()
        factor[rows_of(me), cols] = own_rows[:, cols]

    by_width(me, start_rows)

    def forward_rows(offset):
        def action(cols):
            arrived(offset, cols)
            for b in range(offset.bit_length(), bits):
                far_copy(offset, b, cols).start()
            pass_copy(offset, cols).start()

        by_width(row_block(offset), action)

    owner_step = lax.div(me, n_col)
    place = lax.rem(me, n_col)
    z_rows = pl.ds(pl.multiple_of(place * chunk, 8), chunk)

    def view_cols(v):
        return pl.ds(v * view_width, view_width)

    def chain_step(slots, valid, up, down, recv, d):
        below, above = plane - d, plane + d
        if d:
            @pl.when((below >= 0) & valid(below))
            def _():
                ref = slots(below)
                remote(ref, ref, up.at[d], recv.at[below], me, plane - 1).wait_recv()

        @pl.when((below >= 0) & (plane + 1 < n_col) & valid(below))
        def _():
            ref = slots(below)
            remote(ref, ref, up.at[d], recv.at[below], me, plane + 1).start()

        if d:
            @pl.when((above < n_col) & valid(above))
            def _():
                ref = slots(above)
                remote(ref, ref, down.at[d], recv.at[above], me, plane + 1).wait_recv()

        @pl.when((above < n_col) & (plane > 0) & valid(above))
        def _():
            ref = slots(above)
            remote(ref, ref, down.at[d], recv.at[above], me, plane - 1).start()

    def chain_drain(slots, valid, up, down, recv):
        for d in range(n_col):
            below, above = plane - d, plane + d

            @pl.when((below >= 0) & (plane + 1 < n_col) & valid(below))
            def _():
                ref = slots(below)
                remote(ref, ref, up.at[d], recv.at[below], me, plane + 1).wait_send()

            @pl.when((above < n_col) & (plane > 0) & valid(above))
            def _():
                ref = slots(above)
                remote(ref, ref, down.at[d], recv.at[above], me, plane - 1).wait_send()

    def always(c):
        return c >= 0

    def give_copy(v, c):
        return remote(
            chain.at[v, c], z_full.at[z_rows, view_cols(v)], give_send.at[v, c], give_recv.at[v, place],
            c + n_col * owner_step, plane,
        )

    def give(v, c):
        @pl.when(c == place)
        def _():
            z_full[z_rows, view_cols(v)] = chain[v, c]

        @pl.when(c != place)
        def _():
            give_copy(v, c).start()

    def z_chain(v):
        return functools.partial(lambda v, c: chain.at[v, c], v), always, up_send.at[v], down_send.at[v], chain_recv.at[v]

    def invert():
        by_width(sibling, lambda cols: own_copy(cols).wait_recv())
        for offset in range(1, pairs):
            by_width(row_block(offset) + 1 - 2 * parity, lambda cols: pass_copy(offset, cols).wait_recv())

            def sent(cols):
                for b in range(offset.bit_length(), bits):
                    far_copy(offset, b, cols).wait_send()
                pass_copy(offset, cols).wait_send()

            by_width(row_block(offset), sent)
        if not whole_tile:
            for j in range(width // 128):
                tile = pl.ds(j * 128, 128)
                factor[tile, tile] = base_inverse(factor[tile, tile])
        size = max(sep_rows, 128) if whole_tile else 128
        while size < width:
            for start in range(0, width, 2 * size):
                first, last = pl.ds(start, size), pl.ds(start + size, size)
                inner = dot3(factor[last, first], factor[first, first])
                factor[last, first] = -dot3(factor[last, last], inner)
            size *= 2

        for j in range(width // block):
            depth = pl.ds(j * block, width - j * block)
            here = pl.ds(j * block, block)
            inverse_high[depth, here], inverse_low[depth, here] = halves(factor[depth, here])
            stacked[pl.ds(0, front), here] = dot_pieces(
                (strips_high[:, depth], strips_low[:, depth]), (inverse_high[depth, here], inverse_low[depth, here])
            )
        stacked[pl.ds(front, sep_rows), :] = factor[rows_of(me), :]
        for j in range(width // 128):
            rows = pl.ds(j * 128, 128)
            left_high[rows, :], left_low[rows, :] = halves(stacked[:, rows].T)

    for d in range(n_col):
        if d == n_col - 1:
            for offset in range(n_col, pairs):
                forward_rows(offset)
            invert()
        for v in range(views):
            if d == 0:
                chain[v, plane] = reductions[v][1]()
            chain_step(*z_chain(v), d)

            @pl.when(plane >= d)
            def _():
                give(v, plane - d)

            if d:
                @pl.when(plane + d < n_col)
                def _():
                    give(v, plane + d)

        if d + 1 < min(n_col, pairs):
            forward_rows(d + 1)

    for j in range(n_col):
        @pl.when(j != place)
        def _():
            for v in range(views):
                remote(
                    chain.at[v, plane], z_full.at[pl.ds(j * chunk, chunk), view_cols(v)],
                    give_send.at[v, 0], give_recv.at[v, j], sibling, plane,
                ).wait_recv()

    z_pieces = halves(z_full[...])
    for j in range(width // block):
        depth, here = slice(j * block, width), pl.ds(j * block, block)
        out_update[:, here] = -dot_pieces(
            tuple(piece[:, depth] for piece in z_pieces), (inverse_high[depth, here], inverse_low[depth, here])
        )

    s_views, s_width = s_full.shape[0], s_full.shape[3]
    s_cols = s_views * s_width
    repeat = n_col * s_cols // width
    my_block = lax.div(plane, repeat)
    my_cols = pl.ds(pl.multiple_of(my_block * s_cols, 128), s_cols)
    stacked_y[pl.ds(0, front), :] = -out_update[:, my_cols]
    stacked_y[pl.ds(front, sep_rows), :] = stacked[pl.ds(front, sep_rows), my_cols]
    right = halves(stacked_y[...])
    split = 128 // sep_rows
    for j in range(width // 128):
        rows = pl.ds(j * 128, 128)
        product = dot_pieces((left_high[rows, :], left_low[rows, :]), right)
        for i in range(split):
            q = j * split + i
            for v in range(s_views):
                s_part[v, q % 2, q // 2] = product[
                    i * sep_rows:(i + 1) * sep_rows, v * s_width:(v + 1) * s_width
                ]

    def s_pair_copy(v):
        return remote(s_part.at[v, 1 - parity], s_pair.at[v], s_pair_send.at[v], s_pair_recv.at[v], sibling, plane)

    def first_of_block(c):
        return lax.rem(c, repeat) == 0

    def s_chain(v):
        return (
            functools.partial(lambda v, c: s_full.at[v, lax.div(c, repeat)], v), first_of_block,
            s_up_send.at[v], s_down_send.at[v], s_chain_recv.at[v],
        )

    s_sums = [sums(s_half.at[v], s_in.at[v], s_send.at[v], s_recv.at[v]) for v in range(s_views)]
    for v in range(s_views):
        s_pair_copy(v).start()
    for v in range(s_views):
        s_pair_copy(v).wait_recv()
        s_half[v] = s_part[v, parity] + s_pair[v]
        s_sums[v][0](0)
    for s in range(1, bits):
        for v in range(s_views):
            s_sums[v][0](s)
    for d in range(n_col):
        for v in range(s_views):
            if d == 0:
                total = s_sums[v][1]()

                @pl.when(first_of_block(plane))
                def _():
                    s_full[v, my_block] = total

            chain_step(*s_chain(v), d)
    for j in range(width // s_cols):
        for v in range(s_views):
            out_sep[:, pl.ds(j * s_cols + v * s_width, s_width)] = s_full[v, j]

    for v in range(s_views):
        s_pair_copy(v).wait_send()
        s_sums[v][2]()
        chain_drain(*s_chain(v))
    for v in range(views):
        pair_copy(v).wait_send()
        reductions[v][2]()
        chain_drain(*z_chain(v))
        for c in range(n_col):
            @pl.when(c != place)
            def _():
                give_copy(v, c).wait_send()

    def sent_rows(cols):
        for b in range(bits):
            far_copy(0, b, cols).wait_send()
        own_copy(cols).wait_send()

    by_width(me, sent_rows)


def on_device(parent_sigma, slot_tile, slot_count, panel, sep_factor):
    n_row = lax.axis_size("row")
    n_col = lax.axis_size("col")
    ratio = n_row // n_col
    slot_cap, tile, width = panel.shape[1:]
    front = slot_cap * tile
    sep_rows = sep_factor.shape[0]
    vmem = pl.BlockSpec(memory_space=pltpu.VMEM)
    smem = pl.BlockSpec(memory_space=pltpu.SMEM)
    pairs = n_row // 2
    chunk = ratio * front // n_row
    views = VIEWS
    s_cols = max(128, width // n_col)
    s_views = 2 if s_cols % 256 == 0 else 1
    parts = (views, pairs, chunk, width // views)
    s_parts = (s_views, pairs, sep_rows, s_cols // s_views)
    parent_rows, _, _, parent_cols = parent_sigma.shape[:4]
    sigma = parent_sigma.reshape(parent_rows, tile, parent_cols, tile)
    dma = pltpu.SemaphoreType.DMA
    update, sep = pl.pallas_call(
        functools.partial(main_kernel, n_row, n_col),
        out_shape=(
            jax.ShapeDtypeStruct((front, width), F32),
            jax.ShapeDtypeStruct((sep_rows, width), F32),
        ),
        in_specs=[smem, smem, vmem, vmem, vmem],
        out_specs=(vmem, vmem),
        scratch_shapes=[
            pltpu.VMEM((views, 2) + parts[1:], F32),
            pltpu.VMEM(parts, F32),
            pltpu.VMEM(parts, F32),
            pltpu.VMEM((views, pairs - 1) + parts[2:], F32),
            pltpu.VMEM((views, n_col) + parts[2:], F32),
            pltpu.VMEM((front, width), F32),
            pltpu.VMEM((width, width), F32),
            pltpu.VMEM((sep_rows, width), F32),
            pltpu.VMEM((front, width), BF16),
            pltpu.VMEM((front, width), BF16),
            pltpu.VMEM((width, width), BF16),
            pltpu.VMEM((width, width), BF16),
            pltpu.VMEM((width, front + sep_rows), BF16),
            pltpu.VMEM((width, front + sep_rows), BF16),
            pltpu.VMEM((front + sep_rows, width), F32),
            pltpu.VMEM((front + sep_rows, s_cols), F32),
            pltpu.VMEM((s_views, 2) + s_parts[1:], F32),
            pltpu.VMEM(s_parts, F32),
            pltpu.VMEM(s_parts, F32),
            pltpu.VMEM((s_views, pairs - 1) + s_parts[2:], F32),
            pltpu.VMEM((s_views, width // s_cols) + s_parts[2:], F32),
            dma((views,)), dma((views,)), dma((views, pairs - 1)), dma((views, pairs - 1)),
            dma((1,)), dma((1,)), dma((2 * pairs,)), dma((pairs - 1,)), dma((pairs - 1,)), dma((pairs - 1,)),
            dma((views, n_col)), dma((views, n_col)), dma((views, n_col)),
            dma((views, n_col)), dma((views, n_col)),
            dma((s_views,)), dma((s_views,)), dma((s_views, pairs - 1)), dma((s_views, pairs - 1)),
            dma((s_views, n_col)), dma((s_views, n_col)), dma((s_views, n_col)),
        ],
        compiler_params=pltpu.CompilerParams(
            collective_id=0, has_side_effects=True, vmem_limit_bytes=VMEM_BYTES
        ),
    )(slot_tile, slot_count, sigma, panel, sep_factor)
    return update.reshape(1, slot_cap, tile, width), sep


def solution(mesh):
    placed = (
        P(None, "row", None, None, "col", None),
        P(),
        P(),
        P("row", None, None, None),
        P("row", None),
    )
    return jax.shard_map(
        on_device,
        mesh=mesh,
        in_specs=placed,
        out_specs=(P("row", None, None, None), P("row", None)),
        check_vma=False,
    )
```

```python
import functools

import jax
import jax.numpy as jnp
from jax import lax
from jax.experimental import pallas as pl
from jax.experimental.pallas import tpu as pltpu
from jax.sharding import PartitionSpec as P

MESH = pl.DeviceIdType.MESH
F32 = jnp.float32
BF16 = jnp.bfloat16
VMEM_BYTES = 56 * 1024 * 1024
VIEWS = 2


def halves(x):
    high = x.astype(BF16)
    return high, (x - high.astype(F32)).astype(BF16)


def dot_pieces(left, right):
    (lh, ll), (rh, rl) = left, right
    one = functools.partial(jnp.dot, preferred_element_type=F32)
    return one(lh, rh) + (one(lh, rl) + one(ll, rh))


def dot3(left, right):
    return dot_pieces(halves(left), halves(right))


def base_inverse(block):
    size = block.shape[0]
    row = lax.broadcasted_iota(jnp.int32, block.shape, 0)
    col = lax.broadcasted_iota(jnp.int32, block.shape, 1)
    diagonal = row == col
    inverse = jnp.where(diagonal, 1.0 / jnp.where(diagonal, block, 1.0), 0.0)
    for level in range(size.bit_length() - 1):
        row_block, col_block = row >> level, col >> level
        below = jnp.where((row_block == col_block + 1) & ((row_block & 1) == 1), block, 0.0)
        inverse = inverse - dot3(inverse, dot3(below, inverse))
    return inverse


def main_kernel(
    n_row, n_col, tiles, counts, sigma, panel, sep, out_update, out_sep,
    part, pair_in, half_sum, scatter_in, chain, z_full, factor, diagonals,
    strips_high, strips_low, inverse_high, inverse_low, left_high, left_low, stacked, stacked_y,
    s_part, s_pair, s_half, s_in, s_full,
    pair_send, pair_recv, scatter_send, scatter_recv,
    own_send, own_recv, far_send, far_recv, pass_send, pass_recv, tile_send, tile_recv,
    up_send, down_send, chain_recv, give_send, give_recv,
    s_pair_send, s_pair_recv, s_send, s_recv, s_up_send, s_down_send, s_chain_recv,
):
    me, plane = lax.axis_index("row"), lax.axis_index("col")
    pairs = n_row // 2
    bits = pairs.bit_length() - 1
    parity, mine = lax.rem(me, 2), lax.div(me, 2)
    sibling = me + 1 - 2 * parity
    width = sep.shape[1]
    sep_rows = sep.shape[0]
    slot_cap, tile = panel.shape[1], panel.shape[2]
    front = slot_cap * tile
    ratio = n_row // n_col
    parent_cols = sigma.shape[2]
    chunk = half_sum.shape[2]
    views = half_sum.shape[0]
    view_width = width // views

    def remote(src, dst, send, recv, row, col):
        return pltpu.make_async_remote_copy(
            src_ref=src, dst_ref=dst, send_sem=send, recv_sem=recv,
            device_id=(row, col), device_id_type=MESH,
        )

    barrier = pltpu.get_barrier_semaphore()
    for d in range(1, n_row):
        pl.semaphore_signal(barrier, inc=1, device_id=(lax.rem(me + d, n_row), plane), device_id_type=MESH)
    for d in range(1, n_col):
        pl.semaphore_signal(barrier, inc=1, device_id=(me, lax.rem(plane + d, n_col)), device_id_type=MESH)
    pl.semaphore_wait(barrier, n_row + n_col - 2)

    flip = [(1 - 2 * lax.rem(lax.div(mine, 1 << b), 2)) * (1 << b) for b in range(bits)]
    order = [(1 - parity) * flip[s] + parity * flip[bits - 1 - s] for s in range(bits)]

    def moved(steps, offset):
        pair = mine
        for s in range(bits):
            if offset >> s & 1:
                pair = pair + steps[s]
        return pair

    def sums(held, landed, send, recv):
        def copy(offset):
            s = (offset & -offset).bit_length() - 1
            return remote(
                held.at[moved(order, offset)], landed.at[offset - 1], send.at[offset - 1], recv.at[offset - 1],
                2 * (mine + order[s]) + parity, plane,
            )

        def gathered(offset, s):
            total = held[moved(order, offset)]
            for t in range(s):
                copy(offset | 1 << t).wait_recv()
                total = total + landed[(offset | 1 << t) - 1]
            return total

        def phase(s):
            for offset in reversed(range(1 << s, pairs, 2 << s)):
                if s:
                    held[moved(order, offset)] = gathered(offset, s)
                copy(offset).start()

        def finish():
            return gathered(0, bits)

        def drain():
            for offset in range(1, pairs):
                copy(offset).wait_send()

        return phase, finish, drain

    block = 256
    other_order = order[::-1]

    def rows_of(q):
        return pl.ds(pl.multiple_of(q * sep_rows, 8), sep_rows)

    def by_width(q, action):
        for g in range(width // block):
            @pl.when(lax.div(q * sep_rows, block) == g)
            def _():
                action(pl.ds(0, (g + 1) * block))

    def row_block(offset):
        return 2 * moved(order, offset) + parity

    def sibling_block(offset):
        return 2 * moved(other_order, offset) + 1 - parity

    def own_copy(cols):
        return remote(sep.at[:, cols], factor.at[rows_of(me), cols], own_send.at[0], own_recv.at[0], sibling, plane)

    def far_copy(offset, b, cols):
        rows = rows_of(row_block(offset))
        source = factor.at[rows, cols] if offset else sep.at[:, cols]
        slot = offset + (1 << b) - 1
        return remote(
            source, factor.at[rows, cols], far_send.at[slot], far_recv.at[slot],
            2 * (mine + order[b]) + parity, plane,
        )

    def arrived(offset, cols):
        b = offset.bit_length() - 1
        rows = rows_of(row_block(offset))
        remote(
            factor.at[rows, cols], factor.at[rows, cols], far_send.at[offset - 1], far_recv.at[offset - 1],
            2 * (mine + order[b]) + parity, plane,
        ).wait_recv()

    def pass_copy(q, offset, cols):
        rows = rows_of(q)
        return remote(
            factor.at[rows, cols], factor.at[rows, cols],
            pass_send.at[offset - 1], pass_recv.at[offset - 1], sibling, plane,
        )

    def start_rest(cols):
        for b in range(1, bits):
            far_copy(0, b, cols).start()
        own_copy(cols).start()
        factor[rows_of(me), cols] = sep[:, cols]

    def forward_rows(offset):
        def action(cols):
            arrived(offset, cols)
            for b in range(offset.bit_length(), bits):
                far_copy(offset, b, cols).start()
            pass_copy(row_block(offset), offset, cols).start()

        by_width(row_block(offset), action)

    def tile_own():
        return remote(diagonals.at[me], diagonals.at[me], tile_send.at[0], tile_recv.at[0], sibling, plane)

    def tile_far(offset):
        return remote(
            diagonals.at[me], diagonals.at[me], tile_send.at[offset], tile_recv.at[offset], row_block(offset), plane
        )

    def tile_pass(q, offset):
        slot = pairs - 1 + offset
        return remote(diagonals.at[q], diagonals.at[q], tile_send.at[slot], tile_recv.at[slot], sibling, plane)

    by_width(me, lambda cols: far_copy(0, 0, cols).start())

    def pair_copy(v):
        return remote(part.at[v, 1 - parity], pair_in.at[v], pair_send.at[v], pair_recv.at[v], sibling, plane)

    for s in range(slot_cap):
        live = jnp.where(s < counts[me], 1.0, 0.0).astype(F32)
        rows = pl.ds(s * tile, tile)
        strips_high[rows, :], strips_low[rows, :] = halves(panel[0, s] * live)
    picked = []
    for k in range(ratio * slot_cap):
        step, slot = divmod(k, slot_cap)
        owner = plane + n_col * step
        column = tiles[slot, owner] * ratio + step
        live = jnp.where(slot < counts[owner], 1.0, 0.0).astype(F32)
        stored = [sigma[tiles[s, me], :, column, :] for s in range(slot_cap)]
        picked.append(halves(jnp.concatenate(stored, axis=0).T * live))
    for v in range(views):
        here = pl.ds(v * view_width, view_width)
        right = strips_high[:, here], strips_low[:, here]
        for k in range(ratio * slot_cap):
            product = dot_pieces(picked[k], right)
            for i in range(tile // chunk):
                q = k * (tile // chunk) + i
                part[v, q % 2, q // 2] = product[i * chunk:(i + 1) * chunk]
        pair_copy(v).start()
    for g in range(width // block - 1):
        rest = width - (g + 1) * block
        factor[pl.ds(g * block, block), pl.ds((g + 1) * block, rest)] = jnp.zeros((block, rest), F32)
    reductions = [
        sums(half_sum.at[v], scatter_in.at[v], scatter_send.at[v], scatter_recv.at[v]) for v in range(views)
    ]
    for v in range(views):
        pair_copy(v).wait_recv()
        half_sum[v] = part[v, parity] + pair_in[v]
        reductions[v][0](0)

    whole_tile = sep_rows % 128 == 0
    if whole_tile:
        diagonals[me] = base_inverse(sep[:, pl.ds(pl.multiple_of(me * sep_rows, 128), sep_rows)])
        tile_own().start()
        for offset in range(1, pairs):
            tile_far(offset).start()
    for s in range(1, bits):
        for v in range(views):
            reductions[v][0](s)
    by_width(me, start_rest)

    owner_step = lax.div(me, n_col)
    place = lax.rem(me, n_col)
    z_rows = pl.ds(pl.multiple_of(place * chunk, 8), chunk)

    def view_cols(v):
        return pl.ds(v * view_width, view_width)

    def chain_step(slots, valid, up, down, recv, d):
        below, above = plane - d, plane + d
        if d:
            @pl.when((below >= 0) & valid(below))
            def _():
                ref = slots(below)
                remote(ref, ref, up.at[d], recv.at[below], me, plane - 1).wait_recv()

        @pl.when((below >= 0) & (plane + 1 < n_col) & valid(below))
        def _():
            ref = slots(below)
            remote(ref, ref, up.at[d], recv.at[below], me, plane + 1).start()

        if d:
            @pl.when((above < n_col) & valid(above))
            def _():
                ref = slots(above)
                remote(ref, ref, down.at[d], recv.at[above], me, plane + 1).wait_recv()

        @pl.when((above < n_col) & (plane > 0) & valid(above))
        def _():
            ref = slots(above)
            remote(ref, ref, down.at[d], recv.at[above], me, plane - 1).start()

    def chain_drain(slots, valid, up, down, recv):
        for d in range(n_col):
            below, above = plane - d, plane + d

            @pl.when((below >= 0) & (plane + 1 < n_col) & valid(below))
            def _():
                ref = slots(below)
                remote(ref, ref, up.at[d], recv.at[below], me, plane + 1).wait_send()

            @pl.when((above < n_col) & (plane > 0) & valid(above))
            def _():
                ref = slots(above)
                remote(ref, ref, down.at[d], recv.at[above], me, plane - 1).wait_send()

    def always(c):
        return c >= 0

    def give_copy(v, c):
        return remote(
            chain.at[v, c], z_full.at[z_rows, view_cols(v)], give_send.at[v, c], give_recv.at[v, place],
            c + n_col * owner_step, plane,
        )

    def give(v, c):
        @pl.when(c == place)
        def _():
            z_full[z_rows, view_cols(v)] = chain[v, c]

        @pl.when(c != place)
        def _():
            give_copy(v, c).start()

    def z_chain(v):
        return functools.partial(lambda v, c: chain.at[v, c], v), always, up_send.at[v], down_send.at[v], chain_recv.at[v]

    def invert():
        if whole_tile:
            for offset in range(1, pairs):
                tile_far(offset).wait_recv()
                tile_pass(row_block(offset), offset).start()
        by_width(sibling, lambda cols: own_copy(cols).wait_recv())
        for offset in range(1, pairs):
            by_width(
                sibling_block(offset), lambda cols: pass_copy(sibling_block(offset), offset, cols).wait_recv()
            )

            def sent(cols):
                for b in range(offset.bit_length(), bits):
                    far_copy(offset, b, cols).wait_send()
                pass_copy(row_block(offset), offset, cols).wait_send()

            by_width(row_block(offset), sent)
        if whole_tile:
            tile_own().wait_recv()
            for offset in range(1, pairs):
                tile_pass(sibling_block(offset), offset).wait_recv()
            for q in range(n_row):
                tile_at = pl.ds(q * sep_rows, sep_rows)
                factor[tile_at, tile_at] = diagonals[q]
        else:
            for j in range(width // 128):
                tile = pl.ds(j * 128, 128)
                factor[tile, tile] = base_inverse(factor[tile, tile])
        size = max(sep_rows, 128) if whole_tile else 128
        while size < width:
            for start in range(0, width, 2 * size):
                first, last = pl.ds(start, size), pl.ds(start + size, size)
                inner = dot3(factor[last, first], factor[first, first])
                factor[last, first] = -dot3(factor[last, last], inner)
            size *= 2

        for j in range(width // block):
            depth = pl.ds(j * block, width - j * block)
            here = pl.ds(j * block, block)
            inverse_high[depth, here], inverse_low[depth, here] = halves(factor[depth, here])
            stacked[pl.ds(0, front), here] = dot_pieces(
                (strips_high[:, depth], strips_low[:, depth]), (inverse_high[depth, here], inverse_low[depth, here])
            )
        stacked[pl.ds(front, sep_rows), :] = factor[rows_of(me), :]
        for j in range(width // 128):
            rows = pl.ds(j * 128, 128)
            left_high[rows, :], left_low[rows, :] = halves(stacked[:, rows].T)

    for d in range(n_col):
        if d == n_col - 1:
            for offset in range(n_col, pairs):
                forward_rows(offset)
            invert()
        for v in range(views):
            if d == 0:
                chain[v, plane] = reductions[v][1]()
            chain_step(*z_chain(v), d)

            @pl.when(plane >= d)
            def _():
                give(v, plane - d)

            if d:
                @pl.when(plane + d < n_col)
                def _():
                    give(v, plane + d)

        if d + 1 < min(n_col, pairs):
            forward_rows(d + 1)

    for j in range(n_col):
        @pl.when(j != place)
        def _():
            for v in range(views):
                remote(
                    chain.at[v, plane], z_full.at[pl.ds(j * chunk, chunk), view_cols(v)],
                    give_send.at[v, 0], give_recv.at[v, j], sibling, plane,
                ).wait_recv()

    z_pieces = halves(z_full[...])
    for j in range(width // block):
        depth, here = slice(j * block, width), pl.ds(j * block, block)
        out_update[:, here] = -dot_pieces(
            tuple(piece[:, depth] for piece in z_pieces), (inverse_high[depth, here], inverse_low[depth, here])
        )

    s_views, s_width = s_full.shape[0], s_full.shape[3]
    s_cols = s_views * s_width
    repeat = n_col * s_cols // width
    my_block = lax.div(plane, repeat)
    my_cols = pl.ds(pl.multiple_of(my_block * s_cols, 128), s_cols)
    stacked_y[pl.ds(0, front), :] = -out_update[:, my_cols]
    stacked_y[pl.ds(front, sep_rows), :] = stacked[pl.ds(front, sep_rows), my_cols]
    right = halves(stacked_y[...])
    split = 128 // sep_rows
    for j in range(width // 128):
        rows = pl.ds(j * 128, 128)
        product = dot_pieces((left_high[rows, :], left_low[rows, :]), right)
        for i in range(split):
            q = j * split + i
            for v in range(s_views):
                s_part[v, q % 2, q // 2] = product[
                    i * sep_rows:(i + 1) * sep_rows, v * s_width:(v + 1) * s_width
                ]

    def s_pair_copy(v):
        return remote(s_part.at[v, 1 - parity], s_pair.at[v], s_pair_send.at[v], s_pair_recv.at[v], sibling, plane)

    def first_of_block(c):
        return lax.rem(c, repeat) == 0

    def s_chain(v):
        return (
            functools.partial(lambda v, c: s_full.at[v, lax.div(c, repeat)], v), first_of_block,
            s_up_send.at[v], s_down_send.at[v], s_chain_recv.at[v],
        )

    s_sums = [sums(s_half.at[v], s_in.at[v], s_send.at[v], s_recv.at[v]) for v in range(s_views)]
    for v in range(s_views):
        s_pair_copy(v).start()
    for v in range(s_views):
        s_pair_copy(v).wait_recv()
        s_half[v] = s_part[v, parity] + s_pair[v]
        s_sums[v][0](0)
    for s in range(1, bits):
        for v in range(s_views):
            s_sums[v][0](s)
    for d in range(n_col):
        for v in range(s_views):
            if d == 0:
                total = s_sums[v][1]()

                @pl.when(first_of_block(plane))
                def _():
                    s_full[v, my_block] = total

            chain_step(*s_chain(v), d)
    for j in range(width // s_cols):
        for v in range(s_views):
            out_sep[:, pl.ds(j * s_cols + v * s_width, s_width)] = s_full[v, j]

    for v in range(s_views):
        s_pair_copy(v).wait_send()
        s_sums[v][2]()
        chain_drain(*s_chain(v))
    for v in range(views):
        pair_copy(v).wait_send()
        reductions[v][2]()
        chain_drain(*z_chain(v))
        for c in range(n_col):
            @pl.when(c != place)
            def _():
                give_copy(v, c).wait_send()

    def sent_rows(cols):
        for b in range(bits):
            far_copy(0, b, cols).wait_send()
        own_copy(cols).wait_send()

    by_width(me, sent_rows)
    if whole_tile:
        tile_own().wait_send()
        for offset in range(1, pairs):
            tile_far(offset).wait_send()
            tile_pass(row_block(offset), offset).wait_send()


def hand_over(update, sep, update_out, sep_out, sems):
    parts = 4
    copies = []
    for i, (source, target) in enumerate(((update, update_out), (sep, sep_out))):
        rows = source.shape[0] // parts
        for j in range(parts):
            here = pl.ds(j * rows, rows)
            copy = pltpu.make_async_copy(source.at[here], target.at[here], sems.at[i, j])
            copy.start()
            copies.append(copy)
    for copy in copies:
        copy.wait()


def on_device(parent_sigma, slot_tile, slot_count, panel, sep_factor):
    n_row = lax.axis_size("row")
    n_col = lax.axis_size("col")
    ratio = n_row // n_col
    slot_cap, tile, width = panel.shape[1:]
    front = slot_cap * tile
    sep_rows = sep_factor.shape[0]
    vmem = pl.BlockSpec(memory_space=pltpu.VMEM)
    smem = pl.BlockSpec(memory_space=pltpu.SMEM)
    pairs = n_row // 2
    chunk = ratio * front // n_row
    views = VIEWS
    s_cols = max(128, width // n_col)
    s_views = 2 if s_cols % 256 == 0 else 1
    parts = (views, pairs, chunk, width // views)
    s_parts = (s_views, pairs, sep_rows, s_cols // s_views)
    parent_rows, _, _, parent_cols = parent_sigma.shape[:4]
    sigma = parent_sigma.reshape(parent_rows, tile, parent_cols, tile)
    dma = pltpu.SemaphoreType.DMA
    update, sep = pl.pallas_call(
        functools.partial(main_kernel, n_row, n_col),
        out_shape=(
            jax.ShapeDtypeStruct((front, width), F32),
            jax.ShapeDtypeStruct((sep_rows, width), F32),
        ),
        in_specs=[smem, smem, vmem, vmem, vmem],
        out_specs=(vmem, vmem),
        scratch_shapes=[
            pltpu.VMEM((views, 2) + parts[1:], F32),
            pltpu.VMEM(parts, F32),
            pltpu.VMEM(parts, F32),
            pltpu.VMEM((views, pairs - 1) + parts[2:], F32),
            pltpu.VMEM((views, n_col) + parts[2:], F32),
            pltpu.VMEM((front, width), F32),
            pltpu.VMEM((width, width), F32),
            pltpu.VMEM((n_row, sep_rows, sep_rows), F32),
            pltpu.VMEM((front, width), BF16),
            pltpu.VMEM((front, width), BF16),
            pltpu.VMEM((width, width), BF16),
            pltpu.VMEM((width, width), BF16),
            pltpu.VMEM((width, front + sep_rows), BF16),
            pltpu.VMEM((width, front + sep_rows), BF16),
            pltpu.VMEM((front + sep_rows, width), F32),
            pltpu.VMEM((front + sep_rows, s_cols), F32),
            pltpu.VMEM((s_views, 2) + s_parts[1:], F32),
            pltpu.VMEM(s_parts, F32),
            pltpu.VMEM(s_parts, F32),
            pltpu.VMEM((s_views, pairs - 1) + s_parts[2:], F32),
            pltpu.VMEM((s_views, width // s_cols) + s_parts[2:], F32),
            dma((views,)), dma((views,)), dma((views, pairs - 1)), dma((views, pairs - 1)),
            dma((1,)), dma((1,)), dma((2 * pairs,)), dma((pairs - 1,)), dma((pairs - 1,)), dma((pairs - 1,)),
            dma((2 * pairs - 1,)), dma((2 * pairs - 1,)),
            dma((views, n_col)), dma((views, n_col)), dma((views, n_col)),
            dma((views, n_col)), dma((views, n_col)),
            dma((s_views,)), dma((s_views,)), dma((s_views, pairs - 1)), dma((s_views, pairs - 1)),
            dma((s_views, n_col)), dma((s_views, n_col)), dma((s_views, n_col)),
        ],
        compiler_params=pltpu.CompilerParams(
            collective_id=0, has_side_effects=True, vmem_limit_bytes=VMEM_BYTES
        ),
    )(slot_tile.T, slot_count, sigma, panel, sep_factor)
    anywhere = pl.BlockSpec(memory_space=pl.ANY)
    update, sep = pl.pallas_call(
        hand_over,
        out_shape=(
            jax.ShapeDtypeStruct((front, width), F32),
            jax.ShapeDtypeStruct((sep_rows, width), F32),
        ),
        in_specs=[anywhere] * 2,
        out_specs=(anywhere, anywhere),
        scratch_shapes=[dma((2, 4))],
    )(update, sep)
    return update.reshape(1, slot_cap, tile, width), sep


def solution(mesh):
    placed = (
        P(None, "row", None, None, "col", None),
        P(),
        P(),
        P("row", None, None, None),
        P("row", None),
    )
    return jax.shard_map(
        on_device,
        mesh=mesh,
        in_specs=placed,
        out_specs=(P("row", None, None, None), P("row", None)),
        check_vma=False,
    )
```

```python
import functools

import jax
import jax.numpy as jnp
from jax import lax
from jax.experimental import pallas as pl
from jax.experimental.pallas import tpu as pltpu
from jax.sharding import PartitionSpec as P

MESH = pl.DeviceIdType.MESH
F32 = jnp.float32
BF16 = jnp.bfloat16
VMEM_BYTES = 56 * 1024 * 1024
VIEWS = 4


def halves(x):
    high = x.astype(BF16)
    return high, (x - high.astype(F32)).astype(BF16)


def dot_pieces(left, right):
    (lh, ll), (rh, rl) = left, right
    rows = lh.shape[0]
    both = jnp.dot(jnp.concatenate([lh, ll], axis=0), rh, preferred_element_type=F32)
    return both[:rows] + (both[rows:] + jnp.dot(lh, rl, preferred_element_type=F32))


def dot3(left, right):
    return dot_pieces(halves(left), halves(right))


def base_inverse(block):
    size = block.shape[0]
    row = lax.broadcasted_iota(jnp.int32, block.shape, 0)
    col = lax.broadcasted_iota(jnp.int32, block.shape, 1)
    diagonal = row == col
    inverse = jnp.where(diagonal, 1.0 / jnp.where(diagonal, block, 1.0), 0.0)
    for level in range(size.bit_length() - 1):
        row_block, col_block = row >> level, col >> level
        below = jnp.where((row_block == col_block + 1) & ((row_block & 1) == 1), block, 0.0)
        inverse = inverse - dot3(inverse, dot3(below, inverse))
    return inverse


def main_kernel(
    n_row, n_col, tiles, counts, sigma, panel, sep, out_update, out_sep,
    part, pair_in, half_sum, scatter_in, chain, z_full, factor, diagonals,
    strips_high, strips_low, picked_high, picked_low, inverse_high, inverse_low, left_high, left_low, stacked, stacked_y,
    s_part, s_pair, s_half, s_in, s_full,
    pair_send, pair_recv, scatter_send, scatter_recv,
    own_send, own_recv, far_send, far_recv, pass_send, pass_recv, tile_send, tile_recv,
    up_send, down_send, chain_recv, give_send, give_recv,
    s_pair_send, s_pair_recv, s_send, s_recv, s_up_send, s_down_send, s_chain_recv,
):
    me, plane = lax.axis_index("row"), lax.axis_index("col")
    pairs = n_row // 2
    bits = pairs.bit_length() - 1
    parity, mine = lax.rem(me, 2), lax.div(me, 2)
    sibling = me + 1 - 2 * parity
    width = sep.shape[1]
    sep_rows = sep.shape[0]
    slot_cap, tile = panel.shape[1], panel.shape[2]
    front = slot_cap * tile
    ratio = n_row // n_col
    parent_cols = sigma.shape[2]
    chunk = half_sum.shape[2]
    views = half_sum.shape[0]
    view_width = width // views

    def remote(src, dst, send, recv, row, col):
        return pltpu.make_async_remote_copy(
            src_ref=src, dst_ref=dst, send_sem=send, recv_sem=recv,
            device_id=(row, col), device_id_type=MESH,
        )

    barrier = pltpu.get_barrier_semaphore()
    for d in range(1, n_row):
        pl.semaphore_signal(barrier, inc=1, device_id=(lax.rem(me + d, n_row), plane), device_id_type=MESH)
    for d in range(1, n_col):
        pl.semaphore_signal(barrier, inc=1, device_id=(me, lax.rem(plane + d, n_col)), device_id_type=MESH)
    pl.semaphore_wait(barrier, n_row + n_col - 2)

    flip = [(1 - 2 * lax.rem(lax.div(mine, 1 << b), 2)) * (1 << b) for b in range(bits)]
    order = [(1 - parity) * flip[s] + parity * flip[bits - 1 - s] for s in range(bits)]

    def moved(steps, offset):
        pair = mine
        for s in range(bits):
            if offset >> s & 1:
                pair = pair + steps[s]
        return pair

    def sums(held, landed, send, recv):
        def copy(offset):
            s = (offset & -offset).bit_length() - 1
            return remote(
                held.at[moved(order, offset)], landed.at[offset - 1], send.at[offset - 1], recv.at[offset - 1],
                2 * (mine + order[s]) + parity, plane,
            )

        def gathered(offset, s):
            total = held[moved(order, offset)]
            for t in range(s):
                copy(offset | 1 << t).wait_recv()
                total = total + landed[(offset | 1 << t) - 1]
            return total

        def phase(s):
            for offset in reversed(range(1 << s, pairs, 2 << s)):
                if s:
                    held[moved(order, offset)] = gathered(offset, s)
                copy(offset).start()

        def finish():
            return gathered(0, bits)

        def drain():
            for offset in range(1, pairs):
                copy(offset).wait_send()

        return phase, finish, drain

    block = 256
    other_order = order[::-1]

    def rows_of(q):
        return pl.ds(pl.multiple_of(q * sep_rows, 8), sep_rows)

    def by_width(q, action):
        for g in range(width // block):
            @pl.when(lax.div(q * sep_rows, block) == g)
            def _():
                action(pl.ds(0, (g + 1) * block))

    def row_block(offset):
        return 2 * moved(order, offset) + parity

    def sibling_block(offset):
        return 2 * moved(other_order, offset) + 1 - parity

    def own_copy(cols):
        return remote(sep.at[:, cols], factor.at[rows_of(me), cols], own_send.at[0], own_recv.at[0], sibling, plane)

    def far_copy(offset, b, cols):
        rows = rows_of(row_block(offset))
        source = factor.at[rows, cols] if offset else sep.at[:, cols]
        slot = offset + (1 << b) - 1
        return remote(
            source, factor.at[rows, cols], far_send.at[slot], far_recv.at[slot],
            2 * (mine + order[b]) + parity, plane,
        )

    def arrived(offset, cols):
        b = offset.bit_length() - 1
        rows = rows_of(row_block(offset))
        remote(
            factor.at[rows, cols], factor.at[rows, cols], far_send.at[offset - 1], far_recv.at[offset - 1],
            2 * (mine + order[b]) + parity, plane,
        ).wait_recv()

    def pass_copy(q, offset, cols):
        rows = rows_of(q)
        return remote(
            factor.at[rows, cols], factor.at[rows, cols],
            pass_send.at[offset - 1], pass_recv.at[offset - 1], sibling, plane,
        )

    def start_rest(cols):
        for b in range(1, bits):
            far_copy(0, b, cols).start()
        own_copy(cols).start()
        factor[rows_of(me), cols] = sep[:, cols]

    def forward_rows(offset):
        def action(cols):
            arrived(offset, cols)
            for b in range(offset.bit_length(), bits):
                far_copy(offset, b, cols).start()
            pass_copy(row_block(offset), offset, cols).start()

        by_width(row_block(offset), action)

    def tile_own():
        return remote(diagonals.at[me], diagonals.at[me], tile_send.at[0], tile_recv.at[0], sibling, plane)

    def tile_far(offset):
        return remote(
            diagonals.at[me], diagonals.at[me], tile_send.at[offset], tile_recv.at[offset], row_block(offset), plane
        )

    def tile_pass(q, offset):
        slot = pairs - 1 + offset
        return remote(diagonals.at[q], diagonals.at[q], tile_send.at[slot], tile_recv.at[slot], sibling, plane)

    by_width(me, lambda cols: far_copy(0, 0, cols).start())

    def pair_copy(v):
        return remote(part.at[v, 1 - parity], pair_in.at[v], pair_send.at[v], pair_recv.at[v], sibling, plane)

    for s in range(slot_cap):
        live = jnp.where(s < counts[me], 1.0, 0.0).astype(F32)
        rows = pl.ds(s * tile, tile)
        strips_high[rows, :], strips_low[rows, :] = halves(panel[0, s] * live)
    for k in range(ratio * slot_cap):
        step, slot = divmod(k, slot_cap)
        owner = plane + n_col * step
        column = tiles[slot, owner] * ratio + step
        live = jnp.where(slot < counts[owner], 1.0, 0.0).astype(F32)
        stored = [sigma[tiles[s, me], :, column, :] for s in range(slot_cap)]
        high, low = halves(jnp.concatenate(stored, axis=0).T * live)
        for i in range(tile // chunk):
            q = k * (tile // chunk) + i
            here, rows = pl.ds(q // 2 * chunk, chunk), slice(i * chunk, (i + 1) * chunk)
            picked_high[q % 2, here], picked_low[q % 2, here] = high[rows], low[rows]

    def multiply(side, v):
        here = pl.ds(v * view_width, view_width)
        product = dot_pieces(
            (picked_high[side], picked_low[side]), (strips_high[:, here], strips_low[:, here])
        )
        part[v, side] = product.reshape(pairs, chunk, view_width)

    for v in range(views):
        multiply(1 - parity, v)
        pair_copy(v).start()
    for v in range(views):
        multiply(parity, v)
    for g in range(width // block - 1):
        rest = width - (g + 1) * block
        factor[pl.ds(g * block, block), pl.ds((g + 1) * block, rest)] = jnp.zeros((block, rest), F32)
    reductions = [
        sums(half_sum.at[v], scatter_in.at[v], scatter_send.at[v], scatter_recv.at[v]) for v in range(views)
    ]
    for v in range(views):
        pair_copy(v).wait_recv()
        half_sum[v] = part[v, parity] + pair_in[v]
        reductions[v][0](0)

    for s in range(1, bits):
        for v in range(views):
            reductions[v][0](s)
    by_width(me, start_rest)

    whole_tile = sep_rows % 128 == 0

    def send_tile():
        diagonals[me] = base_inverse(sep[:, pl.ds(pl.multiple_of(me * sep_rows, 128), sep_rows)])
        tile_own().start()
        for offset in range(1, pairs):
            tile_far(offset).start()

    owner_step = lax.div(me, n_col)
    place = lax.rem(me, n_col)
    z_rows = pl.ds(pl.multiple_of(place * chunk, 8), chunk)

    def view_cols(v):
        return pl.ds(v * view_width, view_width)

    def chain_step(slots, valid, up, down, recv, d):
        below, above = plane - d, plane + d
        if d:
            @pl.when((below >= 0) & valid(below))
            def _():
                ref = slots(below)
                remote(ref, ref, up.at[d], recv.at[below], me, plane - 1).wait_recv()

        @pl.when((below >= 0) & (plane + 1 < n_col) & valid(below))
        def _():
            ref = slots(below)
            remote(ref, ref, up.at[d], recv.at[below], me, plane + 1).start()

        if d:
            @pl.when((above < n_col) & valid(above))
            def _():
                ref = slots(above)
                remote(ref, ref, down.at[d], recv.at[above], me, plane + 1).wait_recv()

        @pl.when((above < n_col) & (plane > 0) & valid(above))
        def _():
            ref = slots(above)
            remote(ref, ref, down.at[d], recv.at[above], me, plane - 1).start()

    def chain_drain(slots, valid, up, down, recv):
        for d in range(n_col):
            below, above = plane - d, plane + d

            @pl.when((below >= 0) & (plane + 1 < n_col) & valid(below))
            def _():
                ref = slots(below)
                remote(ref, ref, up.at[d], recv.at[below], me, plane + 1).wait_send()

            @pl.when((above < n_col) & (plane > 0) & valid(above))
            def _():
                ref = slots(above)
                remote(ref, ref, down.at[d], recv.at[above], me, plane - 1).wait_send()

    def always(c):
        return c >= 0

    def give_copy(v, c):
        return remote(
            chain.at[v, c], z_full.at[z_rows, view_cols(v)], give_send.at[v, c], give_recv.at[v, place],
            c + n_col * owner_step, plane,
        )

    def give(v, c):
        @pl.when(c == place)
        def _():
            z_full[z_rows, view_cols(v)] = chain[v, c]

        @pl.when(c != place)
        def _():
            give_copy(v, c).start()

    def z_chain(v):
        return functools.partial(lambda v, c: chain.at[v, c], v), always, up_send.at[v], down_send.at[v], chain_recv.at[v]

    def invert():
        if whole_tile:
            for offset in range(1, pairs):
                tile_far(offset).wait_recv()
                tile_pass(row_block(offset), offset).start()
        by_width(sibling, lambda cols: own_copy(cols).wait_recv())
        for offset in range(1, pairs):
            by_width(
                sibling_block(offset), lambda cols: pass_copy(sibling_block(offset), offset, cols).wait_recv()
            )

            def sent(cols):
                for b in range(offset.bit_length(), bits):
                    far_copy(offset, b, cols).wait_send()
                pass_copy(row_block(offset), offset, cols).wait_send()

            by_width(row_block(offset), sent)
        if whole_tile:
            tile_own().wait_recv()
            for offset in range(1, pairs):
                tile_pass(sibling_block(offset), offset).wait_recv()
            for q in range(n_row):
                tile_at = pl.ds(q * sep_rows, sep_rows)
                factor[tile_at, tile_at] = diagonals[q]
        else:
            for j in range(width // 128):
                tile = pl.ds(j * 128, 128)
                factor[tile, tile] = base_inverse(factor[tile, tile])
        size = max(sep_rows, 128) if whole_tile else 128
        while size < width:
            for start in range(0, width, 2 * size):
                first, last = pl.ds(start, size), pl.ds(start + size, size)
                inner = dot3(factor[last, first], factor[first, first])
                factor[last, first] = -dot3(factor[last, last], inner)
            size *= 2

        for j in range(width // block):
            depth = pl.ds(j * block, width - j * block)
            here = pl.ds(j * block, block)
            inverse_high[depth, here], inverse_low[depth, here] = halves(factor[depth, here])
            stacked[pl.ds(0, front), here] = dot_pieces(
                (strips_high[:, depth], strips_low[:, depth]), (inverse_high[depth, here], inverse_low[depth, here])
            )
        stacked[pl.ds(front, sep_rows), :] = factor[rows_of(me), :]
        split = 128 // sep_rows
        for j in range(width // 128):
            high, low = halves(stacked[:, pl.ds(j * 128, 128)].T)
            for i in range(split):
                q = j * split + i
                rows, here = slice(i * sep_rows, (i + 1) * sep_rows), pl.ds(q // 2 * sep_rows, sep_rows)
                left_high[q % 2, here], left_low[q % 2, here] = high[rows], low[rows]

    for d in range(n_col):
        if d == n_col - 1:
            for offset in range(2, pairs):
                forward_rows(offset)
            invert()
        for v in range(views):
            if d == 0:
                chain[v, plane] = reductions[v][1]()
            chain_step(*z_chain(v), d)

            @pl.when(plane >= d)
            def _():
                give(v, plane - d)

            if d:
                @pl.when(plane + d < n_col)
                def _():
                    give(v, plane + d)

        if d == 0:
            forward_rows(1)
            if whole_tile:
                send_tile()

    for j in range(n_col):
        @pl.when(j != place)
        def _():
            for v in range(views):
                remote(
                    chain.at[v, plane], z_full.at[pl.ds(j * chunk, chunk), view_cols(v)],
                    give_send.at[v, 0], give_recv.at[v, j], sibling, plane,
                ).wait_recv()

    z_pieces = halves(z_full[...])
    for j in range(width // block):
        depth, here = slice(j * block, width), pl.ds(j * block, block)
        out_update[:, here] = -dot_pieces(
            tuple(piece[:, depth] for piece in z_pieces), (inverse_high[depth, here], inverse_low[depth, here])
        )

    s_views, s_width = s_full.shape[0], s_full.shape[3]
    s_cols = s_views * s_width
    repeat = n_col * s_cols // width
    my_block = lax.div(plane, repeat)
    my_cols = pl.ds(pl.multiple_of(my_block * s_cols, 128), s_cols)
    stacked_y[pl.ds(0, front), :] = -out_update[:, my_cols]
    stacked_y[pl.ds(front, sep_rows), :] = stacked[pl.ds(front, sep_rows), my_cols]
    right = halves(stacked_y[...])
    def s_multiply(side):
        product = dot_pieces((left_high[side], left_low[side]), right)
        for v in range(s_views):
            here = slice(v * s_width, (v + 1) * s_width)
            s_part[v, side] = product[:, here].reshape(pairs, sep_rows, s_width)

    def s_pair_copy(v):
        return remote(s_part.at[v, 1 - parity], s_pair.at[v], s_pair_send.at[v], s_pair_recv.at[v], sibling, plane)

    def first_of_block(c):
        return lax.rem(c, repeat) == 0

    def s_chain(v):
        return (
            functools.partial(lambda v, c: s_full.at[v, lax.div(c, repeat)], v), first_of_block,
            s_up_send.at[v], s_down_send.at[v], s_chain_recv.at[v],
        )

    s_sums = [sums(s_half.at[v], s_in.at[v], s_send.at[v], s_recv.at[v]) for v in range(s_views)]
    s_multiply(1 - parity)
    for v in range(s_views):
        s_pair_copy(v).start()
    s_multiply(parity)
    for v in range(s_views):
        s_pair_copy(v).wait_recv()
        s_half[v] = s_part[v, parity] + s_pair[v]
        s_sums[v][0](0)
    for s in range(1, bits):
        for v in range(s_views):
            s_sums[v][0](s)
    for d in range(n_col):
        for v in range(s_views):
            if d == 0:
                total = s_sums[v][1]()

                @pl.when(first_of_block(plane))
                def _():
                    s_full[v, my_block] = total

            chain_step(*s_chain(v), d)
    for j in range(width // s_cols):
        for v in range(s_views):
            out_sep[:, pl.ds(j * s_cols + v * s_width, s_width)] = s_full[v, j]

    for v in range(s_views):
        s_pair_copy(v).wait_send()
        s_sums[v][2]()
        chain_drain(*s_chain(v))
    for v in range(views):
        pair_copy(v).wait_send()
        reductions[v][2]()
        chain_drain(*z_chain(v))
        for c in range(n_col):
            @pl.when(c != place)
            def _():
                give_copy(v, c).wait_send()

    def sent_rows(cols):
        for b in range(bits):
            far_copy(0, b, cols).wait_send()
        own_copy(cols).wait_send()

    by_width(me, sent_rows)
    if whole_tile:
        tile_own().wait_send()
        for offset in range(1, pairs):
            tile_far(offset).wait_send()
            tile_pass(row_block(offset), offset).wait_send()


def on_device(parent_sigma, slot_tile, slot_count, panel, sep_factor):
    n_row = lax.axis_size("row")
    n_col = lax.axis_size("col")
    ratio = n_row // n_col
    slot_cap, tile, width = panel.shape[1:]
    front = slot_cap * tile
    sep_rows = sep_factor.shape[0]
    vmem = pl.BlockSpec(memory_space=pltpu.VMEM)
    smem = pl.BlockSpec(memory_space=pltpu.SMEM)
    pairs = n_row // 2
    chunk = ratio * front // n_row
    views = VIEWS
    s_cols = max(128, width // n_col)
    s_views = 2 if s_cols % 256 == 0 else 1
    parts = (views, pairs, chunk, width // views)
    s_parts = (s_views, pairs, sep_rows, s_cols // s_views)
    parent_rows, _, _, parent_cols = parent_sigma.shape[:4]
    sigma = parent_sigma.reshape(parent_rows, tile, parent_cols, tile)
    dma = pltpu.SemaphoreType.DMA
    update, sep = pl.pallas_call(
        functools.partial(main_kernel, n_row, n_col),
        out_shape=(
            jax.ShapeDtypeStruct((front, width), F32),
            jax.ShapeDtypeStruct((sep_rows, width), F32),
        ),
        in_specs=[smem, smem, vmem, vmem, vmem],
        out_specs=(vmem, vmem),
        scratch_shapes=[
            pltpu.VMEM((views, 2) + parts[1:], F32),
            pltpu.VMEM(parts, F32),
            pltpu.VMEM(parts, F32),
            pltpu.VMEM((views, pairs - 1) + parts[2:], F32),
            pltpu.VMEM((views, n_col) + parts[2:], F32),
            pltpu.VMEM((front, width), F32),
            pltpu.VMEM((width, width), F32),
            pltpu.VMEM((n_row, sep_rows, sep_rows), F32),
            pltpu.VMEM((front, width), BF16),
            pltpu.VMEM((front, width), BF16),
            pltpu.VMEM((2, pairs * chunk, front), BF16),
            pltpu.VMEM((2, pairs * chunk, front), BF16),
            pltpu.VMEM((width, width), BF16),
            pltpu.VMEM((width, width), BF16),
            pltpu.VMEM((2, width // 2, front + sep_rows), BF16),
            pltpu.VMEM((2, width // 2, front + sep_rows), BF16),
            pltpu.VMEM((front + sep_rows, width), F32),
            pltpu.VMEM((front + sep_rows, s_cols), F32),
            pltpu.VMEM((s_views, 2) + s_parts[1:], F32),
            pltpu.VMEM(s_parts, F32),
            pltpu.VMEM(s_parts, F32),
            pltpu.VMEM((s_views, pairs - 1) + s_parts[2:], F32),
            pltpu.VMEM((s_views, width // s_cols) + s_parts[2:], F32),
            dma((views,)), dma((views,)), dma((views, pairs - 1)), dma((views, pairs - 1)),
            dma((1,)), dma((1,)), dma((2 * pairs,)), dma((pairs - 1,)), dma((pairs - 1,)), dma((pairs - 1,)),
            dma((2 * pairs - 1,)), dma((2 * pairs - 1,)),
            dma((views, n_col)), dma((views, n_col)), dma((views, n_col)),
            dma((views, n_col)), dma((views, n_col)),
            dma((s_views,)), dma((s_views,)), dma((s_views, pairs - 1)), dma((s_views, pairs - 1)),
            dma((s_views, n_col)), dma((s_views, n_col)), dma((s_views, n_col)),
        ],
        compiler_params=pltpu.CompilerParams(
            collective_id=0, has_side_effects=True, vmem_limit_bytes=VMEM_BYTES
        ),
    )(slot_tile.T, slot_count, sigma, panel, sep_factor)
    return update.reshape(1, slot_cap, tile, width), sep


def solution(mesh):
    placed = (
        P(None, "row", None, None, "col", None),
        P(),
        P(),
        P("row", None, None, None),
        P("row", None),
    )
    return jax.shard_map(
        on_device,
        mesh=mesh,
        in_specs=placed,
        out_specs=(P("row", None, None, None), P("row", None)),
        check_vma=False,
    )
```

```python
import functools

import jax
import jax.numpy as jnp
from jax import lax
from jax.experimental import pallas as pl
from jax.experimental.pallas import tpu as pltpu
from jax.sharding import PartitionSpec as P

MESH = pl.DeviceIdType.MESH
F32 = jnp.float32
BF16 = jnp.bfloat16
VMEM_BYTES = 56 * 1024 * 1024
VIEWS = 2


def halves(x):
    high = x.astype(BF16)
    return high, (x - high.astype(F32)).astype(BF16)


def dot_pieces(left, right):
    (lh, ll), (rh, rl) = left, right
    rows = lh.shape[0]
    both = jnp.dot(jnp.concatenate([lh, ll], axis=0), rh, preferred_element_type=F32)
    return both[:rows] + (both[rows:] + jnp.dot(lh, rl, preferred_element_type=F32))


def dot3(left, right):
    return dot_pieces(halves(left), halves(right))


def base_inverse(block):
    size = block.shape[0]
    row = lax.broadcasted_iota(jnp.int32, block.shape, 0)
    col = lax.broadcasted_iota(jnp.int32, block.shape, 1)
    diagonal = row == col
    inverse = jnp.where(diagonal, 1.0 / jnp.where(diagonal, block, 1.0), 0.0)
    for level in range(size.bit_length() - 1):
        row_block, col_block = row >> level, col >> level
        below = jnp.where((row_block == col_block + 1) & ((row_block & 1) == 1), block, 0.0)
        inverse = inverse - dot3(inverse, dot3(below, inverse))
    return inverse


def main_kernel(
    n_row, n_col, tiles, counts, sigma, panel, sep, out_update, out_sep,
    part, pair_in, half_sum, scatter_in, chain, z_full, factor, diagonals,
    strips_high, strips_low, picked_high, picked_low, inverse_high, inverse_low, left_high, left_low, stacked, stacked_y,
    s_part, s_pair, s_half, s_in, s_full,
    pair_send, pair_recv, scatter_send, scatter_recv,
    own_send, own_recv, far_send, far_recv, pass_send, pass_recv, tile_send, tile_recv,
    up_send, down_send, chain_recv, give_send, give_recv,
    s_pair_send, s_pair_recv, s_send, s_recv, s_up_send, s_down_send, s_chain_recv,
):
    me, plane = lax.axis_index("row"), lax.axis_index("col")
    pairs = n_row // 2
    bits = pairs.bit_length() - 1
    parity, mine = lax.rem(me, 2), lax.div(me, 2)
    sibling = me + 1 - 2 * parity
    width = sep.shape[1]
    sep_rows = sep.shape[0]
    slot_cap, tile = panel.shape[1], panel.shape[2]
    front = slot_cap * tile
    ratio = n_row // n_col
    parent_cols = sigma.shape[2]
    chunk = half_sum.shape[2]
    views = half_sum.shape[0]
    view_width = width // views

    def remote(src, dst, send, recv, row, col):
        return pltpu.make_async_remote_copy(
            src_ref=src, dst_ref=dst, send_sem=send, recv_sem=recv,
            device_id=(row, col), device_id_type=MESH,
        )

    barrier = pltpu.get_barrier_semaphore()
    for d in range(1, n_row):
        pl.semaphore_signal(barrier, inc=1, device_id=(lax.rem(me + d, n_row), plane), device_id_type=MESH)
    for d in range(1, n_col):
        pl.semaphore_signal(barrier, inc=1, device_id=(me, lax.rem(plane + d, n_col)), device_id_type=MESH)
    pl.semaphore_wait(barrier, n_row + n_col - 2)

    flip = [(1 - 2 * lax.rem(lax.div(mine, 1 << b), 2)) * (1 << b) for b in range(bits)]
    order = [(1 - parity) * flip[s] + parity * flip[bits - 1 - s] for s in range(bits)]

    def moved(steps, offset):
        pair = mine
        for s in range(bits):
            if offset >> s & 1:
                pair = pair + steps[s]
        return pair

    def sums(held, landed, send, recv):
        def copy(offset):
            s = (offset & -offset).bit_length() - 1
            return remote(
                held.at[moved(order, offset)], landed.at[offset - 1], send.at[offset - 1], recv.at[offset - 1],
                2 * (mine + order[s]) + parity, plane,
            )

        def gathered(offset, s):
            total = held[moved(order, offset)]
            for t in range(s):
                copy(offset | 1 << t).wait_recv()
                total = total + landed[(offset | 1 << t) - 1]
            return total

        def phase(s):
            for offset in reversed(range(1 << s, pairs, 2 << s)):
                if s:
                    held[moved(order, offset)] = gathered(offset, s)
                copy(offset).start()

        def finish():
            return gathered(0, bits)

        def drain():
            for offset in range(1, pairs):
                copy(offset).wait_send()

        return phase, finish, drain

    block = 256
    other_order = order[::-1]

    def rows_of(q):
        return pl.ds(pl.multiple_of(q * sep_rows, 8), sep_rows)

    def by_width(q, action):
        for g in range(width // block):
            @pl.when(lax.div(q * sep_rows, block) == g)
            def _():
                action(pl.ds(0, (g + 1) * block))

    def row_block(offset):
        return 2 * moved(order, offset) + parity

    def sibling_block(offset):
        return 2 * moved(other_order, offset) + 1 - parity

    def own_copy(cols):
        return remote(sep.at[:, cols], factor.at[rows_of(me), cols], own_send.at[0], own_recv.at[0], sibling, plane)

    def far_copy(offset, b, cols):
        rows = rows_of(row_block(offset))
        source = factor.at[rows, cols] if offset else sep.at[:, cols]
        slot = offset + (1 << b) - 1
        return remote(
            source, factor.at[rows, cols], far_send.at[slot], far_recv.at[slot],
            2 * (mine + order[b]) + parity, plane,
        )

    def arrived(offset, cols):
        b = offset.bit_length() - 1
        rows = rows_of(row_block(offset))
        remote(
            factor.at[rows, cols], factor.at[rows, cols], far_send.at[offset - 1], far_recv.at[offset - 1],
            2 * (mine + order[b]) + parity, plane,
        ).wait_recv()

    def pass_copy(q, offset, cols):
        rows = rows_of(q)
        return remote(
            factor.at[rows, cols], factor.at[rows, cols],
            pass_send.at[offset - 1], pass_recv.at[offset - 1], sibling, plane,
        )

    def start_rest(cols):
        for b in range(1, bits):
            far_copy(0, b, cols).start()
        own_copy(cols).start()
        factor[rows_of(me), cols] = sep[:, cols]

    def forward_rows(offset):
        def action(cols):
            arrived(offset, cols)
            for b in range(offset.bit_length(), bits):
                far_copy(offset, b, cols).start()
            pass_copy(row_block(offset), offset, cols).start()

        by_width(row_block(offset), action)

    def tile_own():
        return remote(diagonals.at[me], diagonals.at[me], tile_send.at[0], tile_recv.at[0], sibling, plane)

    def tile_far(offset):
        return remote(
            diagonals.at[me], diagonals.at[me], tile_send.at[offset], tile_recv.at[offset], row_block(offset), plane
        )

    def tile_pass(q, offset):
        slot = pairs - 1 + offset
        return remote(diagonals.at[q], diagonals.at[q], tile_send.at[slot], tile_recv.at[slot], sibling, plane)

    by_width(me, lambda cols: far_copy(0, 0, cols).start())

    def pair_copy(v):
        return remote(part.at[v, 1 - parity], pair_in.at[v], pair_send.at[v], pair_recv.at[v], sibling, plane)

    for s in range(slot_cap):
        live = jnp.where(s < counts[me], 1.0, 0.0).astype(F32)
        rows = pl.ds(s * tile, tile)
        strips_high[rows, :], strips_low[rows, :] = halves(panel[0, s] * live)
    for k in range(ratio * slot_cap):
        step, slot = divmod(k, slot_cap)
        owner = plane + n_col * step
        column = tiles[slot, owner] * ratio + step
        live = jnp.where(slot < counts[owner], 1.0, 0.0).astype(F32)
        stored = [sigma[tiles[s, me], :, column, :] for s in range(slot_cap)]
        high, low = halves(jnp.concatenate(stored, axis=0).T * live)
        for i in range(tile // chunk):
            q = k * (tile // chunk) + i
            here, rows = pl.ds(q // 2 * chunk, chunk), slice(i * chunk, (i + 1) * chunk)
            picked_high[q % 2, here], picked_low[q % 2, here] = high[rows], low[rows]

    def multiply(side, v):
        here = pl.ds(v * view_width, view_width)
        product = dot_pieces(
            (picked_high[side], picked_low[side]), (strips_high[:, here], strips_low[:, here])
        )
        part[v, side] = product.reshape(pairs, chunk, view_width)

    for v in range(views):
        multiply(1 - parity, v)
        pair_copy(v).start()
    for v in range(views):
        multiply(parity, v)
    for g in range(width // block - 1):
        rest = width - (g + 1) * block
        factor[pl.ds(g * block, block), pl.ds((g + 1) * block, rest)] = jnp.zeros((block, rest), F32)
    reductions = [
        sums(half_sum.at[v], scatter_in.at[v], scatter_send.at[v], scatter_recv.at[v]) for v in range(views)
    ]
    for v in range(views):
        pair_copy(v).wait_recv()
        half_sum[v] = part[v, parity] + pair_in[v]
        reductions[v][0](0)

    whole_tile = sep_rows % 128 == 0

    def send_tile():
        diagonals[me] = base_inverse(sep[:, pl.ds(pl.multiple_of(me * sep_rows, 128), sep_rows)])
        tile_own().start()
        for offset in range(1, pairs):
            tile_far(offset).start()

    if whole_tile:
        send_tile()
    for s in range(1, bits):
        for v in range(views):
            reductions[v][0](s)
    by_width(me, start_rest)

    owner_step = lax.div(me, n_col)
    place = lax.rem(me, n_col)
    z_rows = pl.ds(pl.multiple_of(place * chunk, 8), chunk)

    def view_cols(v):
        return pl.ds(v * view_width, view_width)

    def chain_step(slots, valid, up, down, recv, d):
        below, above = plane - d, plane + d
        if d:
            @pl.when((below >= 0) & valid(below))
            def _():
                ref = slots(below)
                remote(ref, ref, up.at[d], recv.at[below], me, plane - 1).wait_recv()

        @pl.when((below >= 0) & (plane + 1 < n_col) & valid(below))
        def _():
            ref = slots(below)
            remote(ref, ref, up.at[d], recv.at[below], me, plane + 1).start()

        if d:
            @pl.when((above < n_col) & valid(above))
            def _():
                ref = slots(above)
                remote(ref, ref, down.at[d], recv.at[above], me, plane + 1).wait_recv()

        @pl.when((above < n_col) & (plane > 0) & valid(above))
        def _():
            ref = slots(above)
            remote(ref, ref, down.at[d], recv.at[above], me, plane - 1).start()

    def chain_drain(slots, valid, up, down, recv):
        for d in range(n_col):
            below, above = plane - d, plane + d

            @pl.when((below >= 0) & (plane + 1 < n_col) & valid(below))
            def _():
                ref = slots(below)
                remote(ref, ref, up.at[d], recv.at[below], me, plane + 1).wait_send()

            @pl.when((above < n_col) & (plane > 0) & valid(above))
            def _():
                ref = slots(above)
                remote(ref, ref, down.at[d], recv.at[above], me, plane - 1).wait_send()

    def always(c):
        return c >= 0

    def give_copy(v, c):
        return remote(
            chain.at[v, c], z_full.at[z_rows, view_cols(v)], give_send.at[v, c], give_recv.at[v, place],
            c + n_col * owner_step, plane,
        )

    def give(v, c):
        @pl.when(c == place)
        def _():
            z_full[z_rows, view_cols(v)] = chain[v, c]

        @pl.when(c != place)
        def _():
            give_copy(v, c).start()

    def z_chain(v):
        return functools.partial(lambda v, c: chain.at[v, c], v), always, up_send.at[v], down_send.at[v], chain_recv.at[v]

    def invert():
        if whole_tile:
            for offset in range(1, pairs):
                tile_far(offset).wait_recv()
                tile_pass(row_block(offset), offset).start()
        by_width(sibling, lambda cols: own_copy(cols).wait_recv())
        for offset in range(1, pairs):
            by_width(
                sibling_block(offset), lambda cols: pass_copy(sibling_block(offset), offset, cols).wait_recv()
            )

            def sent(cols):
                for b in range(offset.bit_length(), bits):
                    far_copy(offset, b, cols).wait_send()
                pass_copy(row_block(offset), offset, cols).wait_send()

            by_width(row_block(offset), sent)
        if whole_tile:
            tile_own().wait_recv()
            for offset in range(1, pairs):
                tile_pass(sibling_block(offset), offset).wait_recv()
            for q in range(n_row):
                tile_at = pl.ds(q * sep_rows, sep_rows)
                factor[tile_at, tile_at] = diagonals[q]
        else:
            for j in range(width // 128):
                tile = pl.ds(j * 128, 128)
                factor[tile, tile] = base_inverse(factor[tile, tile])
        size = max(sep_rows, 128) if whole_tile else 128
        while size < width:
            for start in range(0, width, 2 * size):
                first, last = pl.ds(start, size), pl.ds(start + size, size)
                inner = dot3(factor[last, first], factor[first, first])
                factor[last, first] = -dot3(factor[last, last], inner)
            size *= 2

        for j in range(width // block):
            depth = pl.ds(j * block, width - j * block)
            here = pl.ds(j * block, block)
            inverse_high[depth, here], inverse_low[depth, here] = halves(factor[depth, here])
            stacked[pl.ds(0, front), here] = dot_pieces(
                (strips_high[:, depth], strips_low[:, depth]), (inverse_high[depth, here], inverse_low[depth, here])
            )
        stacked[pl.ds(front, sep_rows), :] = factor[rows_of(me), :]
        split = 128 // sep_rows
        for j in range(width // 128):
            high, low = halves(stacked[:, pl.ds(j * 128, 128)].T)
            for i in range(split):
                q = j * split + i
                rows, here = slice(i * sep_rows, (i + 1) * sep_rows), pl.ds(q // 2 * sep_rows, sep_rows)
                left_high[q % 2, here], left_low[q % 2, here] = high[rows], low[rows]

    for d in range(n_col):
        if d == n_col - 1:
            for offset in range(n_col, pairs):
                forward_rows(offset)
            invert()
        for v in range(views):
            if d == 0:
                chain[v, plane] = reductions[v][1]()
            chain_step(*z_chain(v), d)

            @pl.when(plane >= d)
            def _():
                give(v, plane - d)

            if d:
                @pl.when(plane + d < n_col)
                def _():
                    give(v, plane + d)

        if d + 1 < min(n_col, pairs):
            forward_rows(d + 1)

    for j in range(n_col):
        @pl.when(j != place)
        def _():
            for v in range(views):
                remote(
                    chain.at[v, plane], z_full.at[pl.ds(j * chunk, chunk), view_cols(v)],
                    give_send.at[v, 0], give_recv.at[v, j], sibling, plane,
                ).wait_recv()

    z_pieces = halves(z_full[...])
    for j in range(width // block):
        depth, here = slice(j * block, width), pl.ds(j * block, block)
        out_update[:, here] = -dot_pieces(
            tuple(piece[:, depth] for piece in z_pieces), (inverse_high[depth, here], inverse_low[depth, here])
        )

    s_views, s_width = s_full.shape[0], s_full.shape[3]
    s_cols = s_views * s_width
    repeat = n_col * s_cols // width
    my_block = lax.div(plane, repeat)
    my_cols = pl.ds(pl.multiple_of(my_block * s_cols, 128), s_cols)
    stacked_y[pl.ds(0, front), :] = -out_update[:, my_cols]
    stacked_y[pl.ds(front, sep_rows), :] = stacked[pl.ds(front, sep_rows), my_cols]
    right = halves(stacked_y[...])
    def s_multiply(side):
        product = dot_pieces((left_high[side], left_low[side]), right)
        for v in range(s_views):
            here = slice(v * s_width, (v + 1) * s_width)
            s_part[v, side] = product[:, here].reshape(pairs, sep_rows, s_width)

    def s_pair_copy(v):
        return remote(s_part.at[v, 1 - parity], s_pair.at[v], s_pair_send.at[v], s_pair_recv.at[v], sibling, plane)

    def first_of_block(c):
        return lax.rem(c, repeat) == 0

    def s_chain(v):
        return (
            functools.partial(lambda v, c: s_full.at[v, lax.div(c, repeat)], v), first_of_block,
            s_up_send.at[v], s_down_send.at[v], s_chain_recv.at[v],
        )

    s_sums = [sums(s_half.at[v], s_in.at[v], s_send.at[v], s_recv.at[v]) for v in range(s_views)]
    s_multiply(1 - parity)
    for v in range(s_views):
        s_pair_copy(v).start()
    s_multiply(parity)
    for v in range(s_views):
        s_pair_copy(v).wait_recv()
        s_half[v] = s_part[v, parity] + s_pair[v]
        s_sums[v][0](0)
    for s in range(1, bits):
        for v in range(s_views):
            s_sums[v][0](s)
    for d in range(n_col):
        for v in range(s_views):
            if d == 0:
                total = s_sums[v][1]()

                @pl.when(first_of_block(plane))
                def _():
                    s_full[v, my_block] = total

            chain_step(*s_chain(v), d)
    for j in range(width // s_cols):
        for v in range(s_views):
            out_sep[:, pl.ds(j * s_cols + v * s_width, s_width)] = s_full[v, j]

    for v in range(s_views):
        s_pair_copy(v).wait_send()
        s_sums[v][2]()
        chain_drain(*s_chain(v))
    for v in range(views):
        pair_copy(v).wait_send()
        reductions[v][2]()
        chain_drain(*z_chain(v))
        for c in range(n_col):
            @pl.when(c != place)
            def _():
                give_copy(v, c).wait_send()

    def sent_rows(cols):
        for b in range(bits):
            far_copy(0, b, cols).wait_send()
        own_copy(cols).wait_send()

    by_width(me, sent_rows)
    if whole_tile:
        tile_own().wait_send()
        for offset in range(1, pairs):
            tile_far(offset).wait_send()
            tile_pass(row_block(offset), offset).wait_send()


def on_device(parent_sigma, slot_tile, slot_count, panel, sep_factor):
    n_row = lax.axis_size("row")
    n_col = lax.axis_size("col")
    ratio = n_row // n_col
    slot_cap, tile, width = panel.shape[1:]
    front = slot_cap * tile
    sep_rows = sep_factor.shape[0]
    vmem = pl.BlockSpec(memory_space=pltpu.VMEM)
    smem = pl.BlockSpec(memory_space=pltpu.SMEM)
    pairs = n_row // 2
    chunk = ratio * front // n_row
    views = VIEWS
    s_cols = max(128, width // n_col)
    s_views = 2 if s_cols % 256 == 0 else 1
    parts = (views, pairs, chunk, width // views)
    s_parts = (s_views, pairs, sep_rows, s_cols // s_views)
    parent_rows, _, _, parent_cols = parent_sigma.shape[:4]
    sigma = parent_sigma.reshape(parent_rows, tile, parent_cols, tile)
    dma = pltpu.SemaphoreType.DMA
    update, sep = pl.pallas_call(
        functools.partial(main_kernel, n_row, n_col),
        out_shape=(
            jax.ShapeDtypeStruct((front, width), F32),
            jax.ShapeDtypeStruct((sep_rows, width), F32),
        ),
        in_specs=[smem, smem, vmem, vmem, vmem],
        out_specs=(vmem, vmem),
        scratch_shapes=[
            pltpu.VMEM((views, 2) + parts[1:], F32),
            pltpu.VMEM(parts, F32),
            pltpu.VMEM(parts, F32),
            pltpu.VMEM((views, pairs - 1) + parts[2:], F32),
            pltpu.VMEM((views, n_col) + parts[2:], F32),
            pltpu.VMEM((front, width), F32),
            pltpu.VMEM((width, width), F32),
            pltpu.VMEM((n_row, sep_rows, sep_rows), F32),
            pltpu.VMEM((front, width), BF16),
            pltpu.VMEM((front, width), BF16),
            pltpu.VMEM((2, pairs * chunk, front), BF16),
            pltpu.VMEM((2, pairs * chunk, front), BF16),
            pltpu.VMEM((width, width), BF16),
            pltpu.VMEM((width, width), BF16),
            pltpu.VMEM((2, width // 2, front + sep_rows), BF16),
            pltpu.VMEM((2, width // 2, front + sep_rows), BF16),
            pltpu.VMEM((front + sep_rows, width), F32),
            pltpu.VMEM((front + sep_rows, s_cols), F32),
            pltpu.VMEM((s_views, 2) + s_parts[1:], F32),
            pltpu.VMEM(s_parts, F32),
            pltpu.VMEM(s_parts, F32),
            pltpu.VMEM((s_views, pairs - 1) + s_parts[2:], F32),
            pltpu.VMEM((s_views, width // s_cols) + s_parts[2:], F32),
            dma((views,)), dma((views,)), dma((views, pairs - 1)), dma((views, pairs - 1)),
            dma((1,)), dma((1,)), dma((2 * pairs,)), dma((pairs - 1,)), dma((pairs - 1,)), dma((pairs - 1,)),
            dma((2 * pairs - 1,)), dma((2 * pairs - 1,)),
            dma((views, n_col)), dma((views, n_col)), dma((views, n_col)),
            dma((views, n_col)), dma((views, n_col)),
            dma((s_views,)), dma((s_views,)), dma((s_views, pairs - 1)), dma((s_views, pairs - 1)),
            dma((s_views, n_col)), dma((s_views, n_col)), dma((s_views, n_col)),
        ],
        compiler_params=pltpu.CompilerParams(
            collective_id=0, has_side_effects=True, vmem_limit_bytes=VMEM_BYTES
        ),
    )(slot_tile.T, slot_count, sigma, panel, sep_factor)
    return update.reshape(1, slot_cap, tile, width), sep


def solution(mesh):
    placed = (
        P(None, "row", None, None, "col", None),
        P(),
        P(),
        P("row", None, None, None),
        P("row", None),
    )
    return jax.shard_map(
        on_device,
        mesh=mesh,
        in_specs=placed,
        out_specs=(P("row", None, None, None), P("row", None)),
        check_vma=False,
    )
```
